32 devices in a mesh: row: 4 (over y, x), col: 8 (over z, core).
Axes of the slice: x: 2, y: 2, z: 4, core: 2. Of those that a mesh axis runs over, the one named last changes fastest.
Arguments:
- costs: bfloat16 [128, 1024, 128], P('row', 'col'), may hold values from 0 to 63, as said below
- p_small: int32 [1], replicated, may hold values from 4 to 16
- p_large: int32 [1], replicated, may hold values from 32 to 96
Outputs:
- left_view: bfloat16 [128, 1024, 128], P('row', 'col')
- right_view: bfloat16 [128, 1024, 128], P('row', 'col')
The draws below stay inside these ranges and needn't reach their ends.
Inputs may be any that keep to these rules, and one draw needn't show every extreme that they name: `costs`: whole numbers.
All inputs are finite; a program needn't handle non-finite values.
Results may differ from the reference program's by a relative error of at most 0.001.
Values may be sent and summed in bfloat16 or wider, within the bound.
No kernel may reach another device: no remote copies, remote signals or barrier semaphores. Data moves between devices by JAX's collectives and lax.ppermute only.
A program may use at most 64 MiB of HBM per device.

```python
import jax
import jax.numpy as jnp
from jax import lax

DISP = 128
TH = 32
TW = 128
H = 128
W = 1024


def draw_costs(key, part):
    keys = jax.random.split(jax.random.fold_in(key, 7), 8)
    span = DISP // 2
    slope_y = jax.random.randint(keys[0], (), 1, 5)
    slope_x = jax.random.randint(keys[1], (), 1, 5)
    offset_base = jax.random.randint(keys[2], (), 0, 8 * span)
    rows = lax.broadcasted_iota(jnp.int32, (H, W), 0)
    cols = lax.broadcasted_iota(jnp.int32, (H, W), 1)
    target = DISP // 4 + (slope_y * rows + slope_x * cols + offset_base) // 8 % span
    levels = lax.broadcasted_iota(jnp.int32, (1, 1, DISP), 2)
    distance = jnp.abs(levels - target[:, :, None])
    noise_top = 24
    flat_share = 3
    noise = jax.random.randint(keys[3], (H, W, DISP), 0, noise_top)
    textured = jnp.minimum(63, noise + jnp.minimum(48, 4 * distance))
    block_rows = 3 * TH
    block_cols = 3 * TW
    offset_rows = jax.random.randint(keys[4], (), 0, block_rows)
    offset_cols = jax.random.randint(keys[5], (), 0, block_cols)
    flags = jax.random.randint(keys[6], ((H + block_rows) // block_rows + 1, (W + block_cols) // block_cols + 1), 0, 6)
    flat_mask = flags[(rows + offset_rows) // block_rows, (cols + offset_cols) // block_cols] < flat_share
    flat_level = jax.random.randint(keys[7], (H, W), 4, 60)
    values = jnp.where(flat_mask[:, :, None], flat_level[:, :, None], textured)
    return values.astype(jnp.float32).astype(jnp.bfloat16)


def setup_inputs(seed: int = 0) -> dict:
    key_list = jax.random.split(jax.random.key(seed), 4)
    costs = draw_costs(jax.random.fold_in(key_list[3], 71), 0)
    p_small = jax.random.randint(key_list[1], (1,), 4, 17).astype(jnp.int32)
    p_large = jax.random.randint(key_list[2], (1,), 32, 97).astype(jnp.int32)
    return dict(costs=costs, p_small=p_small, p_large=p_large)


def advance(before, here_cost, p_one, p_two):
    lowest = jnp.min(before, axis=-1, keepdims=True)
    barrier = jnp.full(before.shape[:-1] + (1,), jnp.inf, before.dtype)
    lower_side = jnp.concatenate([barrier, before[..., :-1]], axis=-1)
    upper_side = jnp.concatenate([before[..., 1:], barrier], axis=-1)
    smallest = jnp.minimum(jnp.minimum(before, jnp.minimum(lower_side, upper_side) + p_one), lowest + p_two)
    return here_cost + smallest - lowest


def one_path(cost_grid, axis_dim, backward, p_one, p_two):
    moved = jnp.moveaxis(cost_grid, axis_dim, 0)

    def advance_one(before, here_cost):
        after = advance(before, here_cost, p_one, p_two)
        return after, after

    _, values = lax.scan(advance_one, jnp.zeros_like(moved[0]), moved, reverse=backward)
    return jnp.moveaxis(values, 0, axis_dim)


def diagonal_view(joined, out_width):
    row_count, span_count, depth = joined.shape
    turned = jnp.transpose(joined, (0, 2, 1)).reshape(row_count, depth * span_count)
    padded = jnp.pad(turned, ((0, 0), (0, depth)))
    sheared = padded.reshape(row_count, depth, span_count + 1)[:, :, :out_width]
    return jnp.transpose(sheared, (0, 2, 1))


def reference(costs, p_small, p_large):
    cost_grid = costs.astype(jnp.float32)
    p_one = p_small[0].astype(jnp.float32)
    p_two = p_large[0].astype(jnp.float32)
    summed = one_path(cost_grid, 1, False, p_one, p_two)
    summed = summed + one_path(cost_grid, 1, True, p_one, p_two)
    summed = summed + one_path(cost_grid, 0, False, p_one, p_two)
    summed = summed + one_path(cost_grid, 0, True, p_one, p_two)
    left_view = (summed * (1.0 / 64.0)).astype(jnp.bfloat16)
    joined = jnp.pad(left_view, ((0, 0), (0, DISP), (0, 0)))
    right_view = diagonal_view(joined, W)
    return left_view, right_view
```

```python
import functools

import jax
import jax.numpy as jnp
from jax import lax
from jax.experimental import pallas as pl
from jax.experimental.pallas import tpu as pltpu
from jax.sharding import PartitionSpec as P

SUB = 8
BIG = 1e30
TRANSPOSED = (((1,), (1,)), ((), ()))
PLAIN = (((1,), (0,)), ((), ()))
LIMIT = 40 * 1024 * 1024


def one_hot(rule, size):
    row = lax.broadcasted_iota(jnp.int32, (size, size), 0)
    col = lax.broadcasted_iota(jnp.int32, (size, size), 1)
    return jnp.where(rule(row, col), 1.0, 0.0).astype(jnp.bfloat16)


def interleave(size):
    return one_hot(lambda r, c: c == (r % SUB) * (size // SUB) + r // SUB, size)


def identity(size):
    return one_hot(lambda r, c: r == c, size)


def reversal(size):
    return one_hot(lambda r, c: r + c == size - 1, size)


def dot(a, b, dims):
    return lax.dot_general(a, b, dims, preferred_element_type=jnp.float32)


def split(block):
    wide = block.astype(jnp.float32)
    return [wide[i : i + SUB] for i in range(0, wide.shape[0], SUB)]


def join(parts):
    return jnp.concatenate(parts, axis=0).astype(jnp.bfloat16)


def fold_min(parts):
    parts = list(parts)
    while len(parts) > 1:
        parts = [jnp.minimum(a, b) for a, b in zip(parts[::2], parts[1::2])]
    low = parts[0]
    for shift in (4, 2, 1):
        low = jnp.minimum(low, pltpu.roll(low, shift, 0))
    return low


def relax(v, q1, q2):
    sub = lax.broadcasted_iota(jnp.int32, v[0].shape, 0)
    under = jnp.where(sub == 0, BIG, pltpu.roll(v[-1], 1, 0))
    over = jnp.where(sub == SUB - 1, BIG, pltpu.roll(v[0], SUB - 1, 0))
    low = fold_min(v)
    jump = low + q2
    below = [under] + v[:-1]
    above = v[1:] + [over]
    best = [
        jnp.minimum(jnp.minimum(x, jump), jnp.minimum(a, b) + q1)
        for x, a, b in zip(v, below, above)
    ]
    return best, low


def penalties(small_ref, large_ref, lanes):
    shape = (SUB, lanes)
    q1 = jnp.full(shape, small_ref[0], jnp.int32).astype(jnp.float32)
    q2 = jnp.full(shape, large_ref[0], jnp.int32).astype(jnp.float32)
    return q1, q2


def lanes_from(v, fresh, first):
    lane = lax.broadcasted_iota(jnp.int32, v[0].shape, 1)
    return [jnp.where(lane < first, a, b) for a, b in zip(v, fresh)]


def prepare_kernel(costs_ref, turned_ref, out_ref):
    rows, cols, depth = costs_ref.shape
    mix = interleave(depth)
    for g in range(cols // rows):
        span = pl.ds(g * rows, rows)

        def body(y, carry):
            t = g * rows + y
            block = jnp.concatenate(
                [
                    turned_ref[t],
                    turned_ref[cols - 1 - t],
                    costs_ref[y, span, :],
                    costs_ref[rows - 1 - y, span, :],
                ],
                axis=0,
            )
            out_ref[t] = dot(mix, block, TRANSPOSED).astype(jnp.bfloat16)
            return carry

        lax.fori_loop(0, rows, body, 0, unroll=4)


def stage_kernel(rows, small_ref, large_ref, c_ref, h_ref, v_ref, h_out, v_out):
    cols, depth, lanes = c_ref.shape
    q1, q2 = penalties(small_ref, large_ref, lanes)
    v = split(h_ref[...])
    for g in range(cols // rows):
        v = lanes_from(v, split(v_ref[g]), 2 * rows)

        def body(y, v):
            best, _ = relax(list(v), q1, q2)
            return tuple(a + b for a, b in zip(best, split(c_ref[g * rows + y])))

        v = list(lax.fori_loop(0, rows, body, tuple(v), unroll=4))
        low = fold_min(v)
        v = [x - low for x in v]
        v_out[g] = join(v)
    h_out[...] = join(v)


def final_kernel(hops, v_hops, *refs):
    small_ref, large_ref, place_ref, c_ref, costs_ref = refs[:5]
    h_refs = refs[5 : 5 + hops]
    v_refs = refs[5 + hops : 5 + hops + v_hops]
    left_ref, skew_ref, h_sum, v_sum = refs[5 + hops + v_hops :]
    rows, cols, depth = costs_ref.shape
    lanes = c_ref.shape[2]
    q1, q2 = penalties(small_ref, large_ref, lanes)
    col_here, row_here = place_ref[0], place_ref[1]
    lane = lax.broadcasted_iota(jnp.int32, (depth, lanes), 1)
    ident = identity(lanes)

    def pick(arrivals, here, first, second):
        total = jnp.zeros((depth, lanes), jnp.float32)
        count = len(arrivals)
        for s, block in enumerate(arrivals):
            early = jnp.where(here == s + 1, 1.0, 0.0)
            late = jnp.where(here == count - 1 - s, 1.0, 0.0)
            share = jnp.where(lane < first, 0.0, jnp.where(lane < second, early, late))
            total = total + block.astype(jnp.float32) * share
        return split(total)

    v = pick([ref[...] for ref in h_refs], col_here, 0, rows)
    half = rows // 2
    for g in range(cols // rows):
        fresh = pick([ref[g] for ref in v_refs], row_here, 2 * rows, 3 * rows)
        v = lanes_from(v, fresh, 2 * rows)
        for second in (False, True):

            def body(i, v):
                y = i + half if second else i
                t = g * rows + y
                best, low = relax(list(v), q1, q2)
                flat = dot(ident, join([x - low for x in best]), TRANSPOSED)
                spans = [
                    (h_sum, t * rows),
                    (h_sum, (cols - 1 - t) * rows),
                    (v_sum, y * cols + g * rows),
                    (v_sum, (rows - 1 - y) * cols + g * rows),
                ]
                for n, (ref, start) in enumerate(spans):
                    where = pl.ds(pl.multiple_of(start, rows), rows)
                    part = flat[n * rows : (n + 1) * rows]
                    again = 2 * g >= cols // rows if n < 2 else second
                    ref[where, :] = ref[where, :] + part if again else part
                return tuple(a + b for a, b in zip(best, split(c_ref[t])))

            v = list(lax.fori_loop(0, half, body, tuple(v), unroll=2))

    mix = interleave(depth)
    back = reversal(depth)

    def finish(y, carry):
        h_rows = h_sum[pl.ds(y, cols, stride=rows), :].astype(jnp.bfloat16)
        v_rows = v_sum[pl.ds(pl.multiple_of(y * cols, cols), cols), :].astype(jnp.bfloat16)
        extra = dot(h_rows, mix, PLAIN) + dot(v_rows, mix, PLAIN)
        summed = extra + 4.0 * costs_ref[y].astype(jnp.float32)
        left = (summed * (1.0 / 64.0)).astype(jnp.bfloat16)
        left_ref[y] = left
        turned = dot(back, left, TRANSPOSED)
        skewed = pltpu.roll(turned, 1, 1, stride=1, stride_axis=0)
        skewed = dot(ident, skewed.astype(jnp.bfloat16), TRANSPOSED).astype(jnp.bfloat16)
        skew_ref[y] = dot(skewed, back, PLAIN).astype(jnp.bfloat16)
        return carry

    lax.fori_loop(0, rows, finish, 0, unroll=2)


def in_vmem(count):
    return [pl.BlockSpec(memory_space=pltpu.VMEM)] * count


def in_smem(count):
    return [pl.BlockSpec(memory_space=pltpu.SMEM)] * count


def both_ways(block, axis, hop):
    size = lax.axis_size(axis)
    route = [(hop, hop + 1), (size - 1 - hop, size - 2 - hop)]
    return lax.ppermute(block, axis, route)


def shards(costs, p_small, p_large):
    rows, cols, depth = costs.shape
    lanes = 4 * rows
    groups = cols // rows
    col_count, row_count = lax.axis_size("col"), lax.axis_size("row")
    params = pltpu.CompilerParams(vmem_limit_bytes=LIMIT)
    turned = jnp.transpose(costs, (1, 0, 2))
    layered = pl.pallas_call(
        prepare_kernel,
        out_shape=jax.ShapeDtypeStruct((cols, depth, lanes), jnp.bfloat16),
        in_specs=in_vmem(2),
        out_specs=pl.BlockSpec(memory_space=pltpu.VMEM),
        compiler_params=params,
        name="prepare",
    )(costs, turned)

    stage = pl.pallas_call(
        functools.partial(stage_kernel, rows),
        out_shape=(
            jax.ShapeDtypeStruct((depth, lanes), jnp.bfloat16),
            jax.ShapeDtypeStruct((groups, depth, lanes), jnp.bfloat16),
        ),
        in_specs=in_smem(2) + in_vmem(3),
        out_specs=tuple(in_vmem(2)),
        compiler_params=params,
        name="stage",
    )
    h_hops, v_hops = col_count - 1, row_count - 1
    spacing = 2 if 2 * (v_hops - 1) < h_hops else 1
    h_now = jnp.zeros((depth, lanes), jnp.bfloat16)
    v_now = jnp.zeros((groups, depth, lanes), jnp.bfloat16)
    h_got, v_got = [], []
    for s in range(max(h_hops, spacing * (v_hops - 1) + 1)):
        h_end, v_end = stage(p_small, p_large, layered, h_now, v_now)
        if s < h_hops:
            h_now = both_ways(h_end, "col", s)
            h_got.append(h_now)
        if s % spacing == 0 and len(v_got) < v_hops:
            v_next = both_ways(v_end, "row", len(v_got))
            v_got.append(v_next)
        if (s + 1) % spacing == 0:
            v_now = v_next

    place = jnp.stack([lax.axis_index("col"), lax.axis_index("row")]).astype(jnp.int32)
    tile = jax.ShapeDtypeStruct((rows, cols, depth), jnp.bfloat16)
    left_view, skewed = pl.pallas_call(
        functools.partial(final_kernel, h_hops, v_hops),
        out_shape=(tile, tile),
        in_specs=in_smem(3) + in_vmem(2 + h_hops + v_hops),
        out_specs=tuple(in_vmem(2)),
        scratch_shapes=[pltpu.VMEM((rows * cols, depth), jnp.float32)] * 2,
        compiler_params=params,
        name="final",
    )(p_small, p_large, place, layered, costs, *h_got, *v_got)

    arrived = lax.ppermute(skewed, "col", [(i, i - 1) for i in range(1, col_count)])
    x = lax.broadcasted_iota(jnp.int32, (cols, depth), 0)
    d = lax.broadcasted_iota(jnp.int32, (cols, depth), 1)
    right_view = jnp.where((x + d < cols)[None], skewed, arrived)
    return left_view, right_view


def solution(mesh):
    placed = (P("row", "col", None), P(), P())
    return jax.shard_map(
        shards,
        mesh=mesh,
        in_specs=placed,
        out_specs=(P("row", "col", None), P("row", "col", None)),
        check_vma=False,
    )
```

```python
import functools

import jax
import jax.numpy as jnp
from jax import lax
from jax.experimental import pallas as pl
from jax.experimental.pallas import tpu as pltpu
from jax.sharding import PartitionSpec as P

SUB = 8
BIG = 1e30
TRANSPOSED = (((1,), (1,)), ((), ()))
PLAIN = (((1,), (0,)), ((), ()))
LIMIT = 40 * 1024 * 1024


def one_hot(rule, size):
    row = lax.broadcasted_iota(jnp.int32, (size, size), 0)
    col = lax.broadcasted_iota(jnp.int32, (size, size), 1)
    return jnp.where(rule(row, col), 1.0, 0.0).astype(jnp.bfloat16)


def interleave(size):
    return one_hot(lambda r, c: c == (r % SUB) * (size // SUB) + r // SUB, size)


def identity(size):
    return one_hot(lambda r, c: r == c, size)


def dot(a, b, dims):
    return lax.dot_general(a, b, dims, preferred_element_type=jnp.float32)


def split(block):
    wide = block.astype(jnp.float32)
    return [wide[i : i + SUB] for i in range(0, wide.shape[0], SUB)]


def join(parts):
    return jnp.concatenate(parts, axis=0).astype(jnp.bfloat16)


def fold_min(parts):
    parts = list(parts)
    while len(parts) > 1:
        parts = [jnp.minimum(a, b) for a, b in zip(parts[::2], parts[1::2])]
    low = parts[0]
    for shift in (4, 2, 1):
        low = jnp.minimum(low, pltpu.roll(low, shift, 0))
    return low


def relax(v, q1, q2):
    sub = lax.broadcasted_iota(jnp.int32, v[0].shape, 0)
    under = jnp.where(sub == 0, BIG, pltpu.roll(v[-1], 1, 0))
    over = jnp.where(sub == SUB - 1, BIG, pltpu.roll(v[0], SUB - 1, 0))
    low = fold_min(v)
    jump = low + q2
    below = [under] + v[:-1]
    above = v[1:] + [over]
    best = [
        jnp.minimum(jnp.minimum(x, jump), jnp.minimum(a, b) + q1)
        for x, a, b in zip(v, below, above)
    ]
    return best, low


def penalties(small_ref, large_ref, lanes):
    shape = (SUB, lanes)
    q1 = jnp.full(shape, small_ref[0], jnp.int32).astype(jnp.float32)
    q2 = jnp.full(shape, large_ref[0], jnp.int32).astype(jnp.float32)
    return q1, q2


def prepare_kernel(costs_ref, out_ref, wide_ref):
    rows, cols, depth = costs_ref.shape
    mix = interleave(depth)
    batch = 4

    def widen(y, carry):
        where = pl.ds(pl.multiple_of(y * cols, cols), cols)
        wide_ref[where, :] = costs_ref[y].astype(jnp.float32)
        return carry

    lax.fori_loop(0, rows, widen, 0, unroll=4)

    def column(x):
        return wide_ref[pl.ds(x, rows, stride=cols), :].astype(jnp.bfloat16)

    for g in range(cols // rows):
        span = pl.ds(g * rows, rows)

        def body(i, carry):
            parts = []
            for n in range(batch):
                y = i * batch + n
                t = g * rows + y
                parts += [
                    column(t),
                    column(cols - 1 - t),
                    costs_ref[y, span, :],
                    costs_ref[rows - 1 - y, span, :],
                ]
            block = jnp.concatenate(parts, axis=0)
            flat = dot(mix, block, TRANSPOSED).astype(jnp.bfloat16)
            lanes = 4 * rows
            for n in range(batch):
                out_ref[g * rows + i * batch + n] = flat[:, n * lanes : (n + 1) * lanes]
            return carry

        lax.fori_loop(0, rows // batch, body, 0, unroll=2)


def scan(v, c_ref, start, steps, q1, q2, unroll):
    def body(t, v):
        best, _ = relax(list(v), q1, q2)
        return tuple(a + b for a, b in zip(best, split(c_ref[start + t])))

    return list(lax.fori_loop(0, steps, body, tuple(v), unroll=unroll))


def lowered(v):
    low = fold_min(v)
    return [x - low for x in v]


def choose(table, here):
    found = jnp.int32(-1)
    for n, value in enumerate(table):
        found = jnp.where(here == n, jnp.int32(value), found)
    return found


def load_arrival(index, arrivals, held_ref):
    @pl.when(index < 0)
    def _():
        held_ref[...] = jnp.zeros(held_ref.shape, held_ref.dtype)

    for n, ref in enumerate(arrivals):

        @pl.when(index == n)
        def _():
            held_ref[...] = ref[...]


def stage_kernel(plan, s, rows, place_ref, small_ref, large_ref, c_ref, *refs):
    arrivals, out_ref, held_ref = refs[:s], refs[s], refs[s + 1]
    cols, depth, lanes = c_ref.shape
    groups = cols // rows
    col_here, row_here = place_ref[0], place_ref[1]
    q1, q2 = penalties(small_ref, large_ref, lanes)
    across = s < plan.cols - 1
    along = any(s in slots for slots in plan.slots)

    if across:

        @pl.when((col_here == s) | (col_here == plan.cols - 1 - s))
        def _():
            if s:
                v = split(arrivals[s - 1][...])
            else:
                v = [jnp.zeros((SUB, lanes), jnp.float32)] * (depth // SUB)
            v = scan(v, c_ref, 0, cols, q1, q2, 8)
            out_ref[...] = join(lowered(v))

    if along:
        hops = [slots.index(s) if s in slots else -1 for slots in plan.slots]
        source = [slots[j - 1] if j > 0 else -1 for slots, j in zip(plan.slots, hops)]
        hop = choose(hops, col_here)
        south = row_here == hop
        north = row_here == plan.rows - 1 - hop

        @pl.when((hop >= 0) & (south | north))
        def _():
            load_arrival(choose(source, col_here), arrivals, held_ref)
            base = 2 * rows + jnp.where(north, rows, 0)
            lane = lax.broadcasted_iota(jnp.int32, (SUB, lanes), 1)
            packed = None
            for g in range(groups):
                turn = lax.rem(base + lanes - g * rows, lanes)
                v = [pltpu.roll(x, turn, 1) for x in split(held_ref[...])]
                v = lowered(scan(v, c_ref, g * rows, rows, q1, q2, 8))
                turn = lax.rem(lanes - base + g * rows, lanes)
                v = [pltpu.roll(x, turn, 1) for x in v]
                mine = (lane >= g * rows) & (lane < (g + 1) * rows)
                packed = v if packed is None else [jnp.where(mine, a, b) for a, b in zip(v, packed)]
            out_ref[...] = join(packed)


def skew(v, lane, sub):
    count = len(v)
    bit = 1
    while bit < SUB:
        taken = (lane & bit) != 0
        inner = sub < SUB - bit
        up = [pltpu.roll(a, SUB - bit, 0) for a in v]
        v = [
            jnp.where(taken, jnp.where(inner, up[k], up[(k + 1) % count]), v[k])
            for k in range(count)
        ]
        bit *= 2
    while bit < SUB * count:
        taken = (lane & bit) != 0
        v = [jnp.where(taken, v[(k + bit // SUB) % count], v[k]) for k in range(count)]
        bit *= 2
    return v


def final_kernel(plan, stages, *refs):
    place_ref, small_ref, large_ref, c_ref, costs_ref = refs[:5]
    arrivals = refs[5 : 5 + stages]
    left_ref, skew_ref = refs[5 + stages : 7 + stages]
    held_ref, path_ref, east_ref, west_ref, v_ref = refs[7 + stages :]
    rows, cols, depth = costs_ref.shape
    lanes = c_ref.shape[2]
    q1, q2 = penalties(small_ref, large_ref, lanes)
    col_here, row_here = place_ref[0], place_ref[1]
    lane = lax.broadcasted_iota(jnp.int32, (SUB, lanes), 1)
    sub = lax.broadcasted_iota(jnp.int32, (SUB, lanes), 0)

    load_arrival(col_here - 1, arrivals, held_ref.at[0])
    load_arrival(plan.cols - 2 - col_here, arrivals, held_ref.at[1])
    for n in range(2):
        hop = row_here - 1 if n == 0 else plan.rows - 2 - row_here
        source = jnp.int32(-1)
        for j in range(plan.rows - 1):
            found = choose([slots[j] for slots in plan.slots], col_here)
            source = jnp.where(hop == j, found, source)
        load_arrival(source, arrivals, held_ref.at[2 + n])

    east, west = split(held_ref[0]), split(held_ref[1])
    v = [jnp.where(lane < rows, a, b) for a, b in zip(east, west)]
    for g in range(cols // rows):
        south = [pltpu.roll(x, (2 * rows - g * rows) % lanes, 1) for x in split(held_ref[2])]
        north = [pltpu.roll(x, (3 * rows - g * rows) % lanes, 1) for x in split(held_ref[3])]
        fresh = [jnp.where(lane < 3 * rows, a, b) for a, b in zip(south, north)]
        v = [jnp.where(lane < 2 * rows, a, b) for a, b in zip(v, fresh)]

        def body(y, v):
            t = g * rows + y
            best, low = relax(list(v), q1, q2)
            path_ref[t] = join([x - low for x in best])
            return tuple(a + b for a, b in zip(best, split(c_ref[t])))

        v = list(lax.fori_loop(0, rows, body, tuple(v), unroll=8))

    ident = identity(lanes)
    batch = 4
    for g in range(cols // rows):

        def turn(i, carry):
            t = g * rows + i * batch
            block = path_ref[pl.ds(t, batch)].reshape(batch * depth, lanes)
            flat = dot(ident, block, TRANSPOSED)
            for n in range(batch):
                y = i * batch + n
                part = flat[:, n * depth : (n + 1) * depth]
                x = g * rows + y
                east_ref[pl.ds(pl.multiple_of(x * rows, rows), rows), :] = part[:rows]
                x = cols - 1 - x
                west_ref[pl.ds(pl.multiple_of(x * rows, rows), rows), :] = part[rows : 2 * rows]
                v_ref[0, y, g * rows : (g + 1) * rows] = part[2 * rows : 3 * rows]
                v_ref[1, rows - 1 - y, g * rows : (g + 1) * rows] = part[3 * rows :]
            return carry

        lax.fori_loop(0, rows // batch, turn, 0, unroll=2)

    mix = interleave(depth)

    def finish(y, carry):
        crossing = pl.ds(y, cols, stride=rows)
        h_rows = east_ref[crossing, :] + west_ref[crossing, :]
        v_rows = v_ref[0, y] + v_ref[1, y]
        both = jnp.concatenate([h_rows, v_rows], axis=0).astype(jnp.bfloat16)
        extra = dot(both, mix, PLAIN)
        summed = extra[:cols] + extra[cols:] + 4.0 * costs_ref[y].astype(jnp.float32)
        left = (summed * (1.0 / 64.0)).astype(jnp.bfloat16)
        left_ref[y] = left
        skew_ref[y] = join(skew(split(left), lane, sub))
        return carry

    lax.fori_loop(0, rows, finish, 0, unroll=4)


class Plan:
    def __init__(self, rows, cols):
        self.rows, self.cols = rows, cols
        self.slots = []
        for c in range(cols):
            busy = {c - 1, c, cols - 2 - c, cols - 1 - c}
            free = [s for s in range(cols + 4 + rows) if s not in busy or s >= cols - 1]
            self.slots.append(free[: rows - 1])
        last = [slots[-1] + 1 for slots in self.slots if slots]
        self.stages = max([cols - 1] + last)

    def route(self, s):
        pairs = []
        if s < self.cols - 1:
            for r in range(self.rows):
                pairs += [
                    ((r, s), (r, s + 1)),
                    ((r, self.cols - 1 - s), (r, self.cols - 2 - s)),
                ]
        for c, slots in enumerate(self.slots):
            if s in slots:
                j = slots.index(s)
                pairs += [
                    ((j, c), (j + 1, c)),
                    ((self.rows - 1 - j, c), (self.rows - 2 - j, c)),
                ]
        number = lambda place: place[0] * self.cols + place[1]
        return [(number(a), number(b)) for a, b in pairs]


def in_vmem(count):
    return [pl.BlockSpec(memory_space=pltpu.VMEM)] * count


def in_smem(count):
    return [pl.BlockSpec(memory_space=pltpu.SMEM)] * count


def shards(costs, p_small, p_large):
    rows, cols, depth = costs.shape
    lanes = 4 * rows
    plan = Plan(lax.axis_size("row"), lax.axis_size("col"))
    params = pltpu.CompilerParams(vmem_limit_bytes=LIMIT)
    place = jnp.stack([lax.axis_index("col"), lax.axis_index("row")]).astype(jnp.int32)
    layered = pl.pallas_call(
        prepare_kernel,
        out_shape=jax.ShapeDtypeStruct((cols, depth, lanes), jnp.bfloat16),
        in_specs=in_vmem(1),
        out_specs=pl.BlockSpec(memory_space=pltpu.VMEM),
        scratch_shapes=[pltpu.VMEM((rows * cols, depth), jnp.float32)],
        compiler_params=params,
        name="prepare",
    )(costs)

    front = jax.ShapeDtypeStruct((depth, lanes), jnp.bfloat16)
    arrivals = []
    for s in range(plan.stages):
        sent = pl.pallas_call(
            functools.partial(stage_kernel, plan, s, rows),
            out_shape=front,
            in_specs=in_smem(3) + in_vmem(1 + s),
            out_specs=pl.BlockSpec(memory_space=pltpu.VMEM),
            scratch_shapes=[pltpu.VMEM((depth, lanes), jnp.bfloat16)],
            compiler_params=params,
            name=f"stage{s}",
        )(place, p_small, p_large, layered, *arrivals)
        arrivals.append(lax.ppermute(sent, ("row", "col"), plan.route(s)))

    tile = jax.ShapeDtypeStruct((rows, cols, depth), jnp.bfloat16)
    left_view, skewed = pl.pallas_call(
        functools.partial(final_kernel, plan, plan.stages),
        out_shape=(tile, tile),
        in_specs=in_smem(3) + in_vmem(2 + plan.stages),
        out_specs=tuple(in_vmem(2)),
        scratch_shapes=[
            pltpu.VMEM((4, depth, lanes), jnp.bfloat16),
            pltpu.VMEM((cols, depth, lanes), jnp.bfloat16),
            pltpu.VMEM((cols * rows, depth), jnp.float32),
            pltpu.VMEM((cols * rows, depth), jnp.float32),
            pltpu.VMEM((2, rows, cols, depth), jnp.float32),
        ],
        compiler_params=params,
        name="final",
    )(place, p_small, p_large, layered, costs, *arrivals)

    arrived = lax.ppermute(skewed, "col", [(i, i - 1) for i in range(1, plan.cols)])
    x = lax.broadcasted_iota(jnp.int32, (cols, depth), 0)
    d = lax.broadcasted_iota(jnp.int32, (cols, depth), 1)
    right_view = jnp.where((x + d < cols)[None], skewed, arrived)
    return left_view, right_view


def solution(mesh):
    placed = (P("row", "col", None), P(), P())
    return jax.shard_map(
        shards,
        mesh=mesh,
        in_specs=placed,
        out_specs=(P("row", "col", None), P("row", "col", None)),
        check_vma=False,
    )
```

```python
import functools

import jax
import jax.numpy as jnp
from jax import lax
from jax.experimental import pallas as pl
from jax.experimental.pallas import tpu as pltpu
from jax.sharding import PartitionSpec as P

SUB = 8
BIG = 1e30
TRANSPOSED = (((1,), (1,)), ((), ()))
PLAIN = (((1,), (0,)), ((), ()))
LIMIT = 40 * 1024 * 1024


def one_hot(rule, size):
    row = lax.broadcasted_iota(jnp.int32, (size, size), 0)
    col = lax.broadcasted_iota(jnp.int32, (size, size), 1)
    return jnp.where(rule(row, col), 1.0, 0.0).astype(jnp.bfloat16)


def interleave(size):
    return one_hot(lambda r, c: c == (r % SUB) * (size // SUB) + r // SUB, size)


def identity(size):
    return one_hot(lambda r, c: r == c, size)


def dot(a, b, dims):
    return lax.dot_general(a, b, dims, preferred_element_type=jnp.float32)


def split(block):
    wide = block.astype(jnp.float32)
    return [wide[i : i + SUB] for i in range(0, wide.shape[0], SUB)]


def join(parts):
    return jnp.concatenate(parts, axis=0).astype(jnp.bfloat16)


def fold_min(parts):
    parts = list(parts)
    while len(parts) > 1:
        parts = [jnp.minimum(a, b) for a, b in zip(parts[::2], parts[1::2])]
    low = parts[0]
    for shift in (4, 2, 1):
        low = jnp.minimum(low, pltpu.roll(low, shift, 0))
    return low


def relax(v, q1, q2):
    sub = lax.broadcasted_iota(jnp.int32, v[0].shape, 0)
    under = jnp.where(sub == 0, BIG, pltpu.roll(v[-1], 1, 0))
    over = jnp.where(sub == SUB - 1, BIG, pltpu.roll(v[0], SUB - 1, 0))
    low = fold_min(v)
    jump = low + q2
    below = [under] + v[:-1]
    above = v[1:] + [over]
    best = [
        jnp.minimum(jnp.minimum(x, jump), jnp.minimum(a, b) + q1)
        for x, a, b in zip(v, below, above)
    ]
    return best, low


def penalties(small_ref, large_ref, lanes):
    shape = (SUB, lanes)
    q1 = jnp.full(shape, small_ref[0], jnp.int32).astype(jnp.float32)
    q2 = jnp.full(shape, large_ref[0], jnp.int32).astype(jnp.float32)
    return q1, q2


def prepare_kernel(costs_ref, out_ref, wide_ref):
    rows, cols, depth = costs_ref.shape
    pack = cols // rows
    mix = interleave(depth)
    batch = 4

    def widen(y, carry):
        where = pl.ds(pl.multiple_of(y * cols, cols), cols)
        wide_ref[where, :] = costs_ref[y].astype(jnp.float32)
        return carry

    lax.fori_loop(0, rows, widen, 0, unroll=4)

    def body(i, carry):
        parts = [
            wide_ref[pl.ds(i * batch * pack + n, rows, stride=cols), :].astype(jnp.bfloat16)
            for n in range(batch * pack)
        ]
        flat = dot(mix, jnp.concatenate(parts, axis=0), TRANSPOSED).astype(jnp.bfloat16)
        for n in range(batch):
            out_ref[i * batch + n] = flat[:, n * cols : (n + 1) * cols]
        return carry

    lax.fori_loop(0, cols // pack // batch, body, 0, unroll=2)


def turn_rows(costs_ref, tiles_ref):
    rows, cols, depth = costs_ref.shape
    mix = interleave(depth)
    batch = 4

    def body(i, carry):
        block = costs_ref[pl.ds(i * batch, batch)].reshape(batch * cols, depth)
        flat = dot(mix, block, TRANSPOSED).astype(jnp.bfloat16)
        for n in range(batch):
            tiles_ref[i * batch + n] = flat[:, n * cols : (n + 1) * cols]
        return carry

    lax.fori_loop(0, rows // batch, body, 0, unroll=2)


def sweep(v, tiles_ref, sums_ref, rows, west, first, q1, q2):
    tiles, depth, lanes = tiles_ref.shape
    pack = lanes // rows
    lane = lax.broadcasted_iota(jnp.int32, (SUB, lanes), 1)
    groups = [jnp.where(west, pack - 1 - j, j) for j in range(pack)]
    inward = [lax.rem(lanes - g * rows, lanes) for g in groups]
    outward = [g * rows for g in groups]
    mine = [(lane >= g * rows) & (lane < (g + 1) * rows) for g in groups]

    def body(i, v):
        v = list(v)
        at = jnp.where(west, tiles - 1 - i, i)
        tile = split(tiles_ref[at])
        kept = None if first else split(sums_ref[at])
        found = None
        for j in range(pack):
            best, low = relax(v, q1, q2)
            extra = [pltpu.roll(x - low, outward[j], 1) for x in best]
            v = [a + pltpu.roll(c, inward[j], 1) for a, c in zip(best, tile)]
            if found is None:
                found = extra
            else:
                found = [jnp.where(mine[j], a, b) for a, b in zip(extra, found)]
        if kept is not None:
            found = [a + b for a, b in zip(found, kept)]
        sums_ref[at] = join(found)
        return tuple(v)

    return list(lax.fori_loop(0, tiles, body, tuple(v)))


def descend(v, tiles_ref, north, q1, q2):
    rows = tiles_ref.shape[0]

    def body(i, v):
        best, _ = relax(list(v), q1, q2)
        at = jnp.where(north, rows - 1 - i, i)
        return tuple(a + b for a, b in zip(best, split(tiles_ref[at])))

    return list(lax.fori_loop(0, rows, body, tuple(v), unroll=4))


def settle(south, north, costs_ref, tiles_ref, sums_ref, base_ref, q1, q2):
    rows, cols, depth = costs_ref.shape
    count = len(south)

    def both(first, i, v):
        out = []
        for at, part in ((i, v[:count]), (rows - 1 - i, v[count:])):
            best, low = relax(list(part), q1, q2)
            extra = [x - low for x in best]
            if not first:
                extra = [a + b for a, b in zip(extra, split(sums_ref[at]))]
            sums_ref[at] = join(extra)
            out += [a + b for a, b in zip(best, split(tiles_ref[at]))]
        return tuple(out)

    v = lax.fori_loop(0, rows // 2, functools.partial(both, True), tuple(south + north), unroll=2)
    lax.fori_loop(rows // 2, rows, functools.partial(both, False), v, unroll=2)

    ident, mix = identity(cols), interleave(depth)
    batch = 4

    def body(i, carry):
        block = sums_ref[pl.ds(i * batch, batch)].reshape(batch * depth, cols)
        flat = dot(ident, block, TRANSPOSED).astype(jnp.bfloat16)
        for n in range(batch):
            y = i * batch + n
            extra = dot(flat[:, n * depth : (n + 1) * depth], mix, PLAIN)
            base_ref[y] = extra + 4.0 * costs_ref[y].astype(jnp.float32)
        return carry

    lax.fori_loop(0, rows // batch, body, 0, unroll=2)


def lowered(v):
    low = fold_min(v)
    return [x - low for x in v]


def choose(table, here):
    found = jnp.int32(-1)
    for n, value in enumerate(table):
        found = jnp.where(here == n, jnp.int32(value), found)
    return found


def load_arrival(index, arrivals, held_ref):
    @pl.when(index < 0)
    def _():
        held_ref[...] = jnp.zeros(held_ref.shape, held_ref.dtype)

    for n, ref in enumerate(arrivals):

        @pl.when(index == n)
        def _():
            held_ref[...] = ref[...]


def load_verticals(plan, col_here, row_here, arrivals, held_ref):
    for n in range(2):
        hop = row_here - 1 if n == 0 else plan.rows - 2 - row_here
        source = jnp.int32(-1)
        for j in range(plan.rows - 1):
            found = choose([slots[j] for slots in plan.slots], col_here)
            source = jnp.where(hop == j, found, source)
        load_arrival(source, arrivals, held_ref.at[n])


def among(here, columns):
    hit = here == columns[0]
    for c in columns[1:]:
        hit = hit | (here == c)
    return hit


def stage_kernel(plan, s, names, place_ref, small_ref, large_ref, costs_ref, *refs):
    refs = dict(zip(names, refs))
    arrivals = [refs[f"arrival{n}"] for n in range(s)]
    tiles_ref, turned_ref = refs["tiles"], refs["turned"]
    out_ref, held_ref = refs["sent"], refs["held"]
    rows, cols, depth = costs_ref.shape
    col_here, row_here = place_ref[0], place_ref[1]
    q1, q2 = penalties(small_ref, large_ref, cols)

    if s < plan.cols - 1:

        @pl.when((col_here == s) | (col_here == plan.cols - 1 - s))
        def _():
            if s:
                v = split(arrivals[s - 1][...])
            else:
                v = [jnp.zeros((SUB, cols), jnp.float32)] * (depth // SUB)
            west = col_here != s
            v = sweep(v, tiles_ref, refs["sums"], rows, west, 2 * s < plan.cols, q1, q2)
            out_ref[...] = join(lowered(v))

    turning = plan.turning(s)
    if turning:

        @pl.when(among(col_here, turning))
        def _():
            turn_rows(costs_ref, turned_ref)

    if any(s in slots for slots in plan.slots):
        hops = [slots.index(s) if s in slots else -1 for slots in plan.slots]
        source = [slots[j - 1] if j > 0 else -1 for slots, j in zip(plan.slots, hops)]
        hop = choose(hops, col_here)
        north = row_here == plan.rows - 1 - hop

        @pl.when((hop >= 0) & ((row_here == hop) | north))
        def _():
            load_arrival(choose(source, col_here), arrivals, held_ref.at[0])
            v = descend(split(held_ref[0]), turned_ref, north, q1, q2)
            out_ref[...] = join(lowered(v))

    settling = plan.settling(s)
    if settling:

        @pl.when(among(col_here, settling))
        def _():
            load_verticals(plan, col_here, row_here, arrivals, held_ref)
            south, north = split(held_ref[0]), split(held_ref[1])
            settle(south, north, costs_ref, turned_ref, refs["vsums"], refs["base"], q1, q2)


def skew(v, lane, sub):
    count = len(v)
    bit = 1
    while bit < SUB:
        taken = (lane & bit) != 0
        inner = sub < SUB - bit
        up = [pltpu.roll(a, SUB - bit, 0) for a in v]
        v = [
            jnp.where(taken, jnp.where(inner, up[k], up[(k + 1) % count]), v[k])
            for k in range(count)
        ]
        bit *= 2
    while bit < SUB * count:
        taken = (lane & bit) != 0
        v = [jnp.where(taken, v[(k + bit // SUB) % count], v[k]) for k in range(count)]
        bit *= 2
    return v


def unroll_rows(v, sub):
    lanes = v[0].shape[1]
    out = []
    for k, part in enumerate(v):
        if k:
            part = pltpu.roll(part, lanes - k * SUB, 1)
        bit = 1
        while bit < SUB:
            part = jnp.where((sub & bit) != 0, pltpu.roll(part, lanes - bit, 1), part)
            bit *= 2
        out.append(part)
    return out


def final_kernel(plan, names, place_ref, small_ref, large_ref, costs_ref, *refs):
    refs = dict(zip(names, refs))
    arrivals = [refs[f"arrival{n}"] for n in range(plan.stages)]
    rows, cols, depth = costs_ref.shape
    lanes = cols
    held_ref, sums_ref, base_ref, natural_ref = (
        refs["held"], refs["sums"], refs["base"], refs["natural"]
    )
    q1, q2 = penalties(small_ref, large_ref, lanes)
    col_here, row_here = place_ref[0], place_ref[1]

    late = plan.settling(plan.stages)
    if late:

        @pl.when(among(col_here, late))
        def _():
            load_verticals(plan, col_here, row_here, arrivals, held_ref)
            south, north = split(held_ref[0]), split(held_ref[1])
            settle(south, north, costs_ref, refs["turned"], refs["vsums"], base_ref, q1, q2)

    @pl.when((col_here == 0) | (col_here == plan.cols - 1))
    def _():
        v = split(arrivals[plan.cols - 2][...])
        sweep(v, refs["tiles"], sums_ref, rows, col_here == 0, False, q1, q2)

    ident, mix = identity(lanes), interleave(depth)
    batch = 4

    def turn(i, carry):
        block = sums_ref[pl.ds(i * batch, batch)].reshape(batch * depth, lanes)
        flat = dot(ident, block, TRANSPOSED).astype(jnp.bfloat16)
        for n in range(batch):
            at = pl.ds(pl.multiple_of((i * batch + n) * lanes, lanes), lanes)
            natural_ref[at, :] = dot(flat[:, n * depth : (n + 1) * depth], mix, PLAIN)
        return carry

    lax.fori_loop(0, sums_ref.shape[0] // batch, turn, 0, unroll=2)

    lane = lax.broadcasted_iota(jnp.int32, (SUB, lanes), 1)
    sub = lax.broadcasted_iota(jnp.int32, (SUB, lanes), 0)
    half = rows // 2

    def finish(y, carry):
        left, turned = [], []
        for at in (y, y + half):
            across = natural_ref[pl.ds(at, cols, stride=rows), :]
            summed = across + base_ref[at]
            view = (summed * (1.0 / 64.0)).astype(jnp.bfloat16)
            refs["left"][at] = view
            left.append(split(view))
            turned.append(skew(left[-1], lane, sub))
            refs["skewed"][at] = join(turned[-1])
        other = pltpu.roll(jnp.concatenate(turned[1], axis=0), 0, 1, stride=1, stride_axis=0)
        other = [other[i : i + SUB] for i in range(0, cols, SUB)]
        refs["packed"][y] = join(
            [
                jnp.where(lane > sub + k * SUB, a, b)
                for k, (a, b) in enumerate(zip(left[0], other))
            ]
        )
        return carry

    lax.fori_loop(0, half, finish, 0, unroll=2)


def merge_kernel(skewed_ref, packed_ref, right_ref):
    rows, cols, depth = skewed_ref.shape
    lane = lax.broadcasted_iota(jnp.int32, (SUB, depth), 1)
    sub = lax.broadcasted_iota(jnp.int32, (SUB, depth), 0)
    half = rows // 2

    def body(y, carry):
        packed = split(packed_ref[y])
        theirs = [
            skew(packed, lane, sub),
            unroll_rows(packed, sub),
        ]
        for at, other in zip((y, y + half), theirs):
            mine = split(skewed_ref[at])
            right_ref[at] = join(
                [
                    jnp.where(lane + sub + k * SUB < cols, a, b)
                    for k, (a, b) in enumerate(zip(mine, other))
                ]
            )
        return carry

    lax.fori_loop(0, half, body, 0, unroll=2)


class Plan:
    def __init__(self, rows, cols):
        self.rows, self.cols = rows, cols
        self.slots = []
        for c in range(cols):
            busy = {c - 1, c, cols - 2 - c, cols - 1 - c}
            free = [s for s in range(cols + 4 + rows) if s not in busy or s >= cols - 1]
            self.slots.append(free[: rows - 1])
        last = [slots[-1] + 1 for slots in self.slots if slots]
        self.stages = max([cols - 1] + last)

    def route(self, s):
        pairs = []
        if s < self.cols - 1:
            for r in range(self.rows):
                pairs += [
                    ((r, s), (r, s + 1)),
                    ((r, self.cols - 1 - s), (r, self.cols - 2 - s)),
                ]
        for c, slots in enumerate(self.slots):
            if s in slots:
                j = slots.index(s)
                pairs += [
                    ((j, c), (j + 1, c)),
                    ((self.rows - 1 - j, c), (self.rows - 2 - j, c)),
                ]
        number = lambda place: place[0] * self.cols + place[1]
        return [(number(a), number(b)) for a, b in pairs]

    def turning(self, s):
        ends = {0, self.cols - 1}
        return [c for c in range(self.cols) if s == (1 if c in ends else 0)]

    def settling(self, s):
        found = []
        for c, slots in enumerate(self.slots):
            at = slots[-1] + 1
            while at < self.stages and at in (c, self.cols - 1 - c):
                at += 1
            if at == s:
                found.append(c)
        return found


def in_vmem(count):
    return [pl.BlockSpec(memory_space=pltpu.VMEM)] * count


def in_smem(count):
    return [pl.BlockSpec(memory_space=pltpu.SMEM)] * count


def shards(costs, p_small, p_large):
    rows, cols, depth = costs.shape
    plan = Plan(lax.axis_size("row"), lax.axis_size("col"))
    params = {"vmem_limit_bytes": LIMIT}
    place = jnp.stack([lax.axis_index("col"), lax.axis_index("row")]).astype(jnp.int32)
    front = jax.ShapeDtypeStruct((depth, cols), jnp.bfloat16)
    tile = jax.ShapeDtypeStruct((rows, cols, depth), jnp.bfloat16)
    tall = jax.ShapeDtypeStruct((cols * rows // cols, depth, cols), jnp.bfloat16)
    shapes = {
        "sums": tall,
        "turned": jax.ShapeDtypeStruct((rows, depth, cols), jnp.bfloat16),
        "base": jax.ShapeDtypeStruct((rows, cols, depth), jnp.float32),
    }
    held = pltpu.VMEM((2, depth, cols), jnp.bfloat16)
    vsums = pltpu.VMEM((rows, depth, cols), jnp.bfloat16)

    buffers = {
        "tiles": pl.pallas_call(
            prepare_kernel,
            out_shape=tall,
            in_specs=in_vmem(1),
            out_specs=pl.BlockSpec(memory_space=pltpu.VMEM),
            scratch_shapes=[pltpu.VMEM((rows * cols, depth), jnp.float32)],
            compiler_params=pltpu.CompilerParams(**params),
            name="prepare",
        )(costs)
    }

    def run(body, name, results, reads, writes, scratch):
        known = [n for n in writes if n in buffers]
        inputs = reads + known
        outputs = list(results) + writes
        names = [n for n in reads] + [f"{n}_before" for n in known] + outputs + list(scratch)
        lead = 4
        values = pl.pallas_call(
            functools.partial(body, names),
            out_shape=tuple([results[n] for n in results] + [shapes[n] for n in writes]),
            in_specs=in_smem(3) + in_vmem(1 + len(inputs)),
            out_specs=tuple(in_vmem(len(outputs))),
            scratch_shapes=list(scratch.values()),
            input_output_aliases={
                lead + len(reads) + n: outputs.index(name) for n, name in enumerate(known)
            },
            compiler_params=pltpu.CompilerParams(**params),
            name=name,
        )(place, p_small, p_large, costs, *[buffers[n] for n in inputs])
        buffers.update(zip(outputs, values))

    for s in range(plan.stages):
        writes = ["sums"] if s < plan.cols - 1 else []
        writes += ["turned"] if s < 2 else []
        writes += ["base"] if plan.settling(s) else []
        reads = ["tiles"] + ([] if "turned" in writes else ["turned"])
        reads += [f"arrival{n}" for n in range(s)]
        run(
            functools.partial(stage_kernel, plan, s),
            f"stage{s}",
            {"sent": front},
            reads,
            writes,
            {"held": held, "vsums": vsums},
        )
        buffers[f"arrival{s}"] = lax.ppermute(buffers["sent"], ("row", "col"), plan.route(s))

    run(
        functools.partial(final_kernel, plan),
        "final",
        {
            "left": tile,
            "skewed": tile,
            "packed": jax.ShapeDtypeStruct((rows // 2, cols, depth), jnp.bfloat16),
        },
        ["tiles", "turned"] + [f"arrival{n}" for n in range(plan.stages)],
        ["sums", "base"],
        {
            "held": held,
            "vsums": vsums,
            "natural": pltpu.VMEM((cols * rows, depth), jnp.float32),
        },
    )
    arrived = lax.ppermute(buffers["packed"], "col", [(i, i - 1) for i in range(1, plan.cols)])
    right_view = pl.pallas_call(
        merge_kernel,
        out_shape=tile,
        in_specs=in_vmem(2),
        out_specs=pl.BlockSpec(memory_space=pltpu.VMEM),
        compiler_params=pltpu.CompilerParams(**params),
        name="merge",
    )(buffers["skewed"], arrived)
    return buffers["left"], right_view


def solution(mesh):
    placed = (P("row", "col", None), P(), P())
    return jax.shard_map(
        shards,
        mesh=mesh,
        in_specs=placed,
        out_specs=(P("row", "col", None), P("row", "col", None)),
        check_vma=False,
    )
```

```python
import functools

import jax
import jax.numpy as jnp
from jax import lax
from jax.experimental import pallas as pl
from jax.experimental.pallas import tpu as pltpu
from jax.sharding import PartitionSpec as P

SUB = 8
BIG = 1e30
TRANSPOSED = (((1,), (1,)), ((), ()))
PLAIN = (((1,), (0,)), ((), ()))
LIMIT = 40 * 1024 * 1024


def one_hot(rule, size):
    row = lax.broadcasted_iota(jnp.int32, (size, size), 0)
    col = lax.broadcasted_iota(jnp.int32, (size, size), 1)
    return jnp.where(rule(row, col), 1.0, 0.0).astype(jnp.bfloat16)


def interleave(size):
    return one_hot(lambda r, c: c == (r % SUB) * (size // SUB) + r // SUB, size)


def identity(size):
    return one_hot(lambda r, c: r == c, size)


def dot(a, b, dims):
    return lax.dot_general(a, b, dims, preferred_element_type=jnp.float32)


def split(block):
    wide = block.astype(jnp.float32)
    return [wide[i : i + SUB] for i in range(0, wide.shape[0], SUB)]


def join(parts):
    return jnp.concatenate(parts, axis=0).astype(jnp.bfloat16)


def fold_min(parts):
    parts = list(parts)
    while len(parts) > 1:
        parts = [jnp.minimum(a, b) for a, b in zip(parts[::2], parts[1::2])]
    low = parts[0]
    for shift in (4, 2, 1):
        low = jnp.minimum(low, pltpu.roll(low, shift, 0))
    return low


def relax(v, q1, q2):
    sub = lax.broadcasted_iota(jnp.int32, v[0].shape, 0)
    under = jnp.where(sub == 0, BIG, pltpu.roll(v[-1], 1, 0))
    over = jnp.where(sub == SUB - 1, BIG, pltpu.roll(v[0], SUB - 1, 0))
    low = fold_min(v)
    jump = low + q2
    below = [under] + v[:-1]
    above = v[1:] + [over]
    best = [
        jnp.minimum(jnp.minimum(x, jump), jnp.minimum(a, b) + q1)
        for x, a, b in zip(v, below, above)
    ]
    return best, low


def penalties(small_ref, large_ref, lanes):
    shape = (SUB, lanes)
    q1 = jnp.full(shape, small_ref[0], jnp.int32).astype(jnp.float32)
    q2 = jnp.full(shape, large_ref[0], jnp.int32).astype(jnp.float32)
    return q1, q2


def spread(rows, lanes, first):
    row = lax.broadcasted_iota(jnp.int32, (rows * SUB, 2 * lanes), 0)
    col = lax.broadcasted_iota(jnp.int32, (rows * SUB, 2 * lanes), 1)
    hit = row == (col % lanes % rows) * SUB + first + col // lanes
    return jnp.where(hit, 1.0, 0.0).astype(jnp.bfloat16)


def prepare_kernel(costs_ref, out_ref, mixed_ref):
    rows, cols, depth = costs_ref.shape
    mix = interleave(depth)

    def mixed(i, carry):
        at = pl.ds(pl.multiple_of(i * 2 * SUB, 2 * SUB), 2 * SUB)
        wide = costs_ref[:, at, :].astype(jnp.float32)
        for n in range(2):
            part = wide[:, n * SUB : (n + 1) * SUB].reshape(rows * SUB, depth)
            flat = dot(mix, part.astype(jnp.bfloat16), TRANSPOSED)
            mixed_ref[2 * i + n] = flat.astype(jnp.bfloat16)
        return carry

    lax.fori_loop(0, cols // SUB // 2, mixed, 0, unroll=2)
    for j in range(0, SUB, 2):
        pick = spread(rows, cols, j)

        def body(i, carry):
            flat = dot(mixed_ref[i], pick, PLAIN).astype(jnp.bfloat16)
            out_ref[i * SUB + j] = flat[:, :cols]
            out_ref[i * SUB + j + 1] = flat[:, cols:]
            return carry

        lax.fori_loop(0, cols // SUB, body, 0, unroll=4)


def turn_rows(costs_ref, tiles_ref):
    rows, cols, depth = costs_ref.shape
    mix = interleave(depth)
    batch = 4

    def body(i, carry):
        block = costs_ref[pl.ds(i * batch, batch)].reshape(batch * cols, depth)
        flat = dot(mix, block, TRANSPOSED).astype(jnp.bfloat16)
        for n in range(batch):
            tiles_ref[i * batch + n] = flat[:, n * cols : (n + 1) * cols]
        return carry

    lax.fori_loop(0, rows // batch, body, 0, unroll=2)


def sweep(v, tiles_ref, sums_ref, rows, west, first, q1, q2):
    cols, depth, lanes = tiles_ref.shape
    pack = lanes // rows
    lane = lax.broadcasted_iota(jnp.int32, (SUB, lanes), 1)
    groups = [jnp.where(west, pack - 1 - j, j) for j in range(pack)]
    mine = [(lane >= g * rows) & (lane < (g + 1) * rows) for g in groups]

    def body(i, v):
        v = list(v)
        at = jnp.where(west, cols // pack - 1 - i, i)
        found = None
        for j in range(pack):
            best, low = relax(v, q1, q2)
            extra = [x - low for x in best]
            v = [a + c for a, c in zip(best, split(tiles_ref[at * pack + groups[j]]))]
            if found is None:
                found = extra
            else:
                found = [jnp.where(mine[j], a, b) for a, b in zip(extra, found)]
        if not first:
            found = [a + b for a, b in zip(found, split(sums_ref[at]))]
        sums_ref[at] = join(found)
        return tuple(v)

    return list(lax.fori_loop(0, cols // pack, body, tuple(v)))


def descend(v, tiles_ref, north, q1, q2):
    rows = tiles_ref.shape[0]

    def body(i, v):
        best, _ = relax(list(v), q1, q2)
        at = jnp.where(north, rows - 1 - i, i)
        return tuple(a + b for a, b in zip(best, split(tiles_ref[at])))

    return list(lax.fori_loop(0, rows, body, tuple(v), unroll=4))


def settle(south, north, costs_ref, tiles_ref, sums_ref, base_ref, q1, q2):
    rows, cols, depth = costs_ref.shape
    count = len(south)

    def both(first, i, v):
        out = []
        for at, part in ((i, v[:count]), (rows - 1 - i, v[count:])):
            best, low = relax(list(part), q1, q2)
            extra = [x - low for x in best]
            if not first:
                extra = [a + b for a, b in zip(extra, split(sums_ref[at]))]
            sums_ref[at] = join(extra)
            out += [a + b for a, b in zip(best, split(tiles_ref[at]))]
        return tuple(out)

    v = lax.fori_loop(0, rows // 2, functools.partial(both, True), tuple(south + north), unroll=2)
    lax.fori_loop(rows // 2, rows, functools.partial(both, False), v, unroll=2)

    ident, mix = identity(cols), interleave(depth)
    batch = 4

    def body(i, carry):
        block = sums_ref[pl.ds(i * batch, batch)].reshape(batch * depth, cols)
        flat = dot(ident, block, TRANSPOSED).astype(jnp.bfloat16)
        for n in range(batch):
            y = i * batch + n
            extra = dot(flat[:, n * depth : (n + 1) * depth], mix, PLAIN)
            base_ref[y] = extra + 4.0 * costs_ref[y].astype(jnp.float32)
        return carry

    lax.fori_loop(0, rows // batch, body, 0, unroll=2)


def lowered(v):
    low = fold_min(v)
    return [x - low for x in v]


def choose(table, here):
    found = jnp.int32(-1)
    for n, value in enumerate(table):
        found = jnp.where(here == n, jnp.int32(value), found)
    return found


def load_arrival(index, arrivals, held_ref):
    @pl.when(index < 0)
    def _():
        held_ref[...] = jnp.zeros(held_ref.shape, held_ref.dtype)

    for n, ref in enumerate(arrivals):

        @pl.when(index == n)
        def _():
            held_ref[...] = ref[...]


def load_verticals(plan, col_here, row_here, arrivals, held_ref):
    for n in range(2):
        hop = row_here - 1 if n == 0 else plan.rows - 2 - row_here
        source = jnp.int32(-1)
        for j in range(plan.rows - 1):
            found = choose([slots[j] for slots in plan.slots], col_here)
            source = jnp.where(hop == j, found, source)
        load_arrival(source, arrivals, held_ref.at[n])


def among(here, columns):
    hit = here == columns[0]
    for c in columns[1:]:
        hit = hit | (here == c)
    return hit


def stage_kernel(plan, s, names, place_ref, small_ref, large_ref, costs_ref, *refs):
    refs = dict(zip(names, refs))
    arrivals = [refs[f"arrival{n}"] for n in range(s)]
    tiles_ref, turned_ref = refs["tiles"], refs["turned"]
    out_ref, held_ref = refs["sent"], refs["held"]
    rows, cols, depth = costs_ref.shape
    col_here, row_here = place_ref[0], place_ref[1]
    q1, q2 = penalties(small_ref, large_ref, cols)

    if s < plan.cols - 1:

        @pl.when((col_here == s) | (col_here == plan.cols - 1 - s))
        def _():
            west = col_here != s
            if s:
                v = split(arrivals[s - 1][...])
            else:
                v = [jnp.zeros((SUB, cols), jnp.float32)] * (depth // SUB)
            if plan.crossing(s - 1):
                other = split(refs["crossed"][...])
                v = [jnp.where(west, b, a) for a, b in zip(v, other)]
            v = sweep(v, tiles_ref, refs["sums"], rows, west, 2 * s < plan.cols, q1, q2)
            out_ref[...] = join(lowered(v))

    turning = plan.turning(s)
    if turning:

        @pl.when(among(col_here, turning))
        def _():
            turn_rows(costs_ref, turned_ref)

    if any(s in slots for slots in plan.slots):
        hops = [slots.index(s) if s in slots else -1 for slots in plan.slots]
        source = [slots[j - 1] if j > 0 else -1 for slots, j in zip(plan.slots, hops)]
        hop = choose(hops, col_here)
        north = row_here == plan.rows - 1 - hop

        @pl.when((hop >= 0) & ((row_here == hop) | north))
        def _():
            load_arrival(choose(source, col_here), arrivals, held_ref.at[0])
            v = descend(split(held_ref[0]), turned_ref, north, q1, q2)
            out_ref[...] = join(lowered(v))

    settling = plan.settling(s)
    if settling:

        @pl.when(among(col_here, settling))
        def _():
            load_verticals(plan, col_here, row_here, arrivals, held_ref)
            south, north = split(held_ref[0]), split(held_ref[1])
            settle(south, north, costs_ref, turned_ref, refs["vsums"], refs["base"], q1, q2)


def skew(v, lane, sub):
    count = len(v)
    bit = 1
    while bit < SUB:
        taken = (lane & bit) != 0
        inner = sub < SUB - bit
        up = [pltpu.roll(a, SUB - bit, 0) for a in v]
        v = [
            jnp.where(taken, jnp.where(inner, up[k], up[(k + 1) % count]), v[k])
            for k in range(count)
        ]
        bit *= 2
    while bit < SUB * count:
        taken = (lane & bit) != 0
        v = [jnp.where(taken, v[(k + bit // SUB) % count], v[k]) for k in range(count)]
        bit *= 2
    return v


def final_kernel(plan, names, place_ref, small_ref, large_ref, costs_ref, *refs):
    refs = dict(zip(names, refs))
    arrivals = [refs[f"arrival{n}"] for n in range(plan.stages)]
    rows, cols, depth = costs_ref.shape
    lanes = cols
    held_ref, sums_ref, base_ref, natural_ref = (
        refs["held"], refs["sums"], refs["base"], refs["natural"]
    )
    q1, q2 = penalties(small_ref, large_ref, lanes)
    col_here, row_here = place_ref[0], place_ref[1]

    late = plan.settling(plan.stages)
    if late:

        @pl.when(among(col_here, late))
        def _():
            load_verticals(plan, col_here, row_here, arrivals, held_ref)
            south, north = split(held_ref[0]), split(held_ref[1])
            settle(south, north, costs_ref, refs["turned"], refs["vsums"], base_ref, q1, q2)

    @pl.when((col_here == 0) | (col_here == plan.cols - 1))
    def _():
        v = split(arrivals[plan.cols - 2][...])
        sweep(v, refs["tiles"], sums_ref, rows, col_here == 0, False, q1, q2)

    order, mix = interleave(2 * cols), interleave(depth)

    def turn(i, carry):
        pair = jnp.concatenate([sums_ref[2 * i], sums_ref[2 * i + 1]], axis=1)
        flat = dot(order, pair, TRANSPOSED).astype(jnp.bfloat16)
        at = pl.ds(pl.multiple_of(i * SUB, SUB), SUB)
        natural_ref[:, at, :] = dot(flat, mix, PLAIN).reshape(rows, SUB, depth)
        return carry

    lax.fori_loop(0, cols // SUB, turn, 0, unroll=4)

    lane = lax.broadcasted_iota(jnp.int32, (SUB, lanes), 1)
    sub = lax.broadcasted_iota(jnp.int32, (SUB, lanes), 0)
    half = rows // 2
    middle = cols // SUB // 2

    def finish(y, carry):
        turned = []
        for at in (y, y + half):
            summed = natural_ref[at] + base_ref[at]
            view = (summed * (1.0 / 64.0)).astype(jnp.bfloat16)
            refs["left"][at] = view
            turned.append(skew(split(view), lane, sub))
            refs["skewed"][at] = join(turned[-1])
        corner = [
            jnp.where(lane >= lanes // 2, a, pltpu.roll(b, lanes // 2, 1))
            for a, b in zip(turned[0][:middle], turned[1][:middle])
        ]
        refs["packed"][y] = join(corner + turned[0][middle:] + turned[1][middle:])
        return carry

    lax.fori_loop(0, half, finish, 0, unroll=2)


def merge_kernel(skewed_ref, packed_ref, right_ref):
    rows, cols, depth = skewed_ref.shape
    lane = lax.broadcasted_iota(jnp.int32, (SUB, depth), 1)
    sub = lax.broadcasted_iota(jnp.int32, (SUB, depth), 0)
    half = rows // 2
    middle = cols // SUB // 2

    def body(y, carry):
        packed = split(packed_ref[y])
        corner = packed[:middle]
        theirs = [
            corner + packed[middle : 2 * middle],
            [pltpu.roll(x, depth // 2, 1) for x in corner] + packed[2 * middle :],
        ]
        for at, other in zip((y, y + half), theirs):
            mine = split(skewed_ref[at])
            right_ref[at] = join(
                [
                    jnp.where(lane + sub + k * SUB < cols, a, b)
                    for k, (a, b) in enumerate(zip(mine, other))
                ]
            )
        return carry

    lax.fori_loop(0, half, body, 0, unroll=2)


class Plan:
    def __init__(self, rows, cols):
        self.rows, self.cols = rows, cols
        self.slots = []
        for c in range(cols):
            busy = {c - 1, c, cols - 2 - c, cols - 1 - c}
            free = [s for s in range(cols + 4 + rows) if s not in busy or s >= cols - 1]
            self.slots.append(free[: rows - 1])
        last = [slots[-1] + 1 for slots in self.slots if slots]
        self.stages = max([cols - 1] + last)

    def crossing(self, s):
        return 2 * s == self.cols - 2

    def numbers(self, pairs):
        number = lambda place: place[0] * self.cols + place[1]
        return [(number(a), number(b)) for a, b in pairs]

    def crossed_route(self, s):
        return self.numbers([((r, s + 1), (r, s)) for r in range(self.rows)])

    def route(self, s):
        pairs = []
        if s < self.cols - 1:
            for r in range(self.rows):
                pairs.append(((r, s), (r, s + 1)))
                if not self.crossing(s):
                    pairs.append(((r, self.cols - 1 - s), (r, self.cols - 2 - s)))
        for c, slots in enumerate(self.slots):
            if s in slots:
                j = slots.index(s)
                pairs += [
                    ((j, c), (j + 1, c)),
                    ((self.rows - 1 - j, c), (self.rows - 2 - j, c)),
                ]
        return self.numbers(pairs)

    def turning(self, s):
        ends = {0, self.cols - 1}
        return [c for c in range(self.cols) if s == (1 if c in ends else 0)]

    def settling(self, s):
        found = []
        for c, slots in enumerate(self.slots):
            at = slots[-1] + 1
            while at < self.stages and at in (c, self.cols - 1 - c):
                at += 1
            if at == s:
                found.append(c)
        return found


def in_vmem(count):
    return [pl.BlockSpec(memory_space=pltpu.VMEM)] * count


def in_smem(count):
    return [pl.BlockSpec(memory_space=pltpu.SMEM)] * count


def shards(costs, p_small, p_large):
    rows, cols, depth = costs.shape
    plan = Plan(lax.axis_size("row"), lax.axis_size("col"))
    params = {"vmem_limit_bytes": LIMIT}
    place = jnp.stack([lax.axis_index("col"), lax.axis_index("row")]).astype(jnp.int32)
    front = jax.ShapeDtypeStruct((depth, cols), jnp.bfloat16)
    tile = jax.ShapeDtypeStruct((rows, cols, depth), jnp.bfloat16)
    shapes = {
        "sums": jax.ShapeDtypeStruct((rows, depth, cols), jnp.bfloat16),
        "turned": jax.ShapeDtypeStruct((rows, depth, cols), jnp.bfloat16),
        "base": jax.ShapeDtypeStruct((rows, cols, depth), jnp.float32),
    }
    held = pltpu.VMEM((2, depth, cols), jnp.bfloat16)
    vsums = pltpu.VMEM((rows, depth, cols), jnp.bfloat16)

    buffers = {
        "tiles": pl.pallas_call(
            prepare_kernel,
            out_shape=jax.ShapeDtypeStruct((cols, depth, cols), jnp.bfloat16),
            in_specs=in_vmem(1),
            out_specs=pl.BlockSpec(memory_space=pltpu.VMEM),
            scratch_shapes=[pltpu.VMEM((cols // SUB, depth, rows * SUB), jnp.bfloat16)],
            compiler_params=pltpu.CompilerParams(**params),
            name="prepare",
        )(costs)
    }

    def run(body, name, results, reads, writes, scratch):
        known = [n for n in writes if n in buffers]
        inputs = reads + known
        outputs = list(results) + writes
        names = [n for n in reads] + [f"{n}_before" for n in known] + outputs + list(scratch)
        lead = 4
        values = pl.pallas_call(
            functools.partial(body, names),
            out_shape=tuple([results[n] for n in results] + [shapes[n] for n in writes]),
            in_specs=in_smem(3) + in_vmem(1 + len(inputs)),
            out_specs=tuple(in_vmem(len(outputs))),
            scratch_shapes=list(scratch.values()),
            input_output_aliases={
                lead + len(reads) + n: outputs.index(name) for n, name in enumerate(known)
            },
            compiler_params=pltpu.CompilerParams(**params),
            name=name,
        )(place, p_small, p_large, costs, *[buffers[n] for n in inputs])
        buffers.update(zip(outputs, values))

    for s in range(plan.stages):
        writes = ["sums"] if s < plan.cols - 1 else []
        writes += ["turned"] if s < 2 else []
        writes += ["base"] if plan.settling(s) else []
        reads = ["tiles"] + ([] if "turned" in writes else ["turned"])
        reads += [f"arrival{n}" for n in range(s)]
        reads += ["crossed"] if plan.crossing(s - 1) else []
        run(
            functools.partial(stage_kernel, plan, s),
            f"stage{s}",
            {"sent": front},
            reads,
            writes,
            {"held": held, "vsums": vsums},
        )
        buffers[f"arrival{s}"] = lax.ppermute(buffers["sent"], ("row", "col"), plan.route(s))
        if plan.crossing(s):
            route = plan.crossed_route(s)
            buffers["crossed"] = lax.ppermute(buffers["sent"], ("row", "col"), route)

    run(
        functools.partial(final_kernel, plan),
        "final",
        {
            "left": tile,
            "skewed": tile,
            "packed": jax.ShapeDtypeStruct((rows // 2, cols // 2 * 3, depth), jnp.bfloat16),
        },
        ["tiles", "turned"] + [f"arrival{n}" for n in range(plan.stages)],
        ["sums", "base"],
        {
            "held": held,
            "vsums": vsums,
            "natural": pltpu.VMEM((rows, cols, depth), jnp.float32),
        },
    )
    arrived = lax.ppermute(buffers["packed"], "col", [(i, i - 1) for i in range(1, plan.cols)])
    right_view = pl.pallas_call(
        merge_kernel,
        out_shape=tile,
        in_specs=in_vmem(2),
        out_specs=pl.BlockSpec(memory_space=pltpu.VMEM),
        compiler_params=pltpu.CompilerParams(**params),
        name="merge",
    )(buffers["skewed"], arrived)
    return buffers["left"], right_view


def solution(mesh):
    placed = (P("row", "col", None), P(), P())
    return jax.shard_map(
        shards,
        mesh=mesh,
        in_specs=placed,
        out_specs=(P("row", "col", None), P("row", "col", None)),
        check_vma=False,
    )
```

```python
import functools

import jax
import jax.numpy as jnp
from jax import lax
from jax.experimental import pallas as pl
from jax.experimental.pallas import tpu as pltpu
from jax.sharding import PartitionSpec as P

SUB = 8
BIG = 1e30
TRANSPOSED = (((1,), (1,)), ((), ()))
PLAIN = (((1,), (0,)), ((), ()))
LIMIT = 20 * 1024 * 1024


def one_hot(rule, size):
    row = lax.broadcasted_iota(jnp.int32, (size, size), 0)
    col = lax.broadcasted_iota(jnp.int32, (size, size), 1)
    return jnp.where(rule(row, col), 1.0, 0.0).astype(jnp.bfloat16)


def interleave(size):
    return one_hot(lambda r, c: c == (r % SUB) * (size // SUB) + r // SUB, size)


def identity(size):
    return one_hot(lambda r, c: r == c, size)


def dot(a, b, dims):
    return lax.dot_general(a, b, dims, preferred_element_type=jnp.float32)


def split(block):
    wide = block.astype(jnp.float32)
    return [wide[i : i + SUB] for i in range(0, wide.shape[0], SUB)]


def join(parts):
    return jnp.concatenate(parts, axis=0).astype(jnp.bfloat16)


def fold_min(parts):
    parts = list(parts)
    while len(parts) > 1:
        parts = [jnp.minimum(a, b) for a, b in zip(parts[::2], parts[1::2])]
    low = parts[0]
    for shift in (4, 2, 1):
        low = jnp.minimum(low, pltpu.roll(low, shift, 0))
    return low


def relax(v, q1, q2):
    sub = lax.broadcasted_iota(jnp.int32, v[0].shape, 0)
    under = jnp.where(sub == 0, BIG, pltpu.roll(v[-1], 1, 0))
    over = jnp.where(sub == SUB - 1, BIG, pltpu.roll(v[0], SUB - 1, 0))
    low = fold_min(v)
    jump = low + q2
    below = [under] + v[:-1]
    above = v[1:] + [over]
    best = [
        jnp.minimum(jnp.minimum(x, jump), jnp.minimum(a, b) + q1)
        for x, a, b in zip(v, below, above)
    ]
    return best, low


def penalties(prices_ref):
    return prices_ref[0], prices_ref[1]


def spread(rows, lanes, first):
    row = lax.broadcasted_iota(jnp.int32, (rows * SUB, 2 * lanes), 0)
    col = lax.broadcasted_iota(jnp.int32, (rows * SUB, 2 * lanes), 1)
    hit = row == (col % lanes % rows) * SUB + first + col // lanes
    return jnp.where(hit, 1.0, 0.0).astype(jnp.bfloat16)


def prepare_kernel(
    costs_ref, small_ref, large_ref,
    out_ref, low_ref, prices_ref, near_ref,
    mixed_ref, price_refs, arrived,
):
    rows, cols, depth = costs_ref.shape
    mix = interleave(depth)
    fetches = [
        pltpu.make_async_copy(ref, price_refs.at[n], arrived.at[n])
        for n, ref in enumerate((small_ref, large_ref))
    ]
    for fetch in fetches:
        fetch.start()

    def mixed(i, carry):
        at = pl.ds(pl.multiple_of(i * 2 * SUB, 2 * SUB), 2 * SUB)
        block = costs_ref[:, at, :]
        near_ref[:, at, :] = block
        wide = block.astype(jnp.float32)
        for n in range(2):
            part = wide[:, n * SUB : (n + 1) * SUB].reshape(rows * SUB, depth)
            flat = dot(mix, part.astype(jnp.bfloat16), TRANSPOSED)
            mixed_ref[2 * i + n] = flat.astype(jnp.bfloat16)
        return carry

    lax.fori_loop(0, cols // SUB // 2, mixed, 0, unroll=2)
    for j in range(0, SUB, 2):
        pick = spread(rows, cols, j)

        def body(i, carry):
            flat = dot(mixed_ref[i], pick, PLAIN)
            for n in range(2):
                part = flat[:, n * cols : (n + 1) * cols]
                out_ref[i * SUB + j + n] = part
                low_ref[i * SUB + j + n] = fold_min(split(part))
            return carry

        lax.fori_loop(0, cols // SUB, body, 0, unroll=4)

    for n, fetch in enumerate(fetches):
        fetch.wait()
        price = jnp.full(prices_ref.shape[1:], price_refs[n, 0], jnp.int32)
        prices_ref[n] = price.astype(jnp.float32)


def turn_rows(costs_ref, tiles_ref):
    rows, cols, depth = costs_ref.shape
    mix = interleave(depth)
    batch = 4

    def body(i, carry):
        block = costs_ref[pl.ds(i * batch, batch)].reshape(batch * cols, depth)
        flat = dot(mix, block, TRANSPOSED).astype(jnp.bfloat16)
        for n in range(batch):
            tiles_ref[i * batch + n] = flat[:, n * cols : (n + 1) * cols]
        return carry

    lax.fori_loop(0, rows // batch, body, 0, unroll=2)


def sweep(v, tiles_ref, lows_ref, sums_ref, rows, west, first, q1, q2):
    cols, depth, lanes = tiles_ref.shape
    pack = lanes // rows
    lane = lax.broadcasted_iota(jnp.int32, (SUB, lanes), 1)
    sub = lax.broadcasted_iota(jnp.int32, (SUB, lanes), 0)
    groups = [jnp.where(west, pack - 1 - j, j) for j in range(pack)]
    mine = [(lane >= g * rows) & (lane < (g + 1) * rows) for g in groups]

    def body(i, carry):
        v, jump = list(carry[:-1]), carry[-1]
        at = jnp.where(west, cols // pack - 1 - i, i)
        found = None
        for j in range(pack):
            x = at * pack + groups[j]
            c = split(tiles_ref[x])
            below = [jnp.where(sub == 0, BIG, pltpu.roll(v[-1], 1, 0))] + v[:-1]
            above = v[1:] + [jnp.where(sub == SUB - 1, BIG, pltpu.roll(v[0], SUB - 1, 0))]
            near = [
                jnp.minimum(n, jnp.minimum(a, b) + q1) + k
                for n, a, b, k in zip(v, below, above, c)
            ]
            far = [k + jump for k in c]
            v = [jnp.minimum(a, b) for a, b in zip(near, far)]
            jump = jnp.minimum(fold_min(near), lows_ref[x] + jump) + q2
            extra = [a - b for a, b in zip(v, far)]
            if found is None:
                found = extra
            else:
                found = [jnp.where(mine[j], a, b) for a, b in zip(extra, found)]
        if not first:
            found = [a + b for a, b in zip(found, split(sums_ref[at]))]
        sums_ref[at] = join(found)
        return tuple(v) + (jump,)

    last = lax.fori_loop(0, cols // pack, body, tuple(v) + (fold_min(v) + q2,))
    low = last[-1] - q2
    return [x - low for x in last[:-1]]


def descend(v, tiles_ref, north, q1, q2):
    rows = tiles_ref.shape[0]

    def body(i, v):
        best, _ = relax(list(v), q1, q2)
        at = jnp.where(north, rows - 1 - i, i)
        return tuple(a + b for a, b in zip(best, split(tiles_ref[at])))

    return list(lax.fori_loop(0, rows, body, tuple(v), unroll=4))


def settle(south, north, costs_ref, tiles_ref, sums_ref, base_ref, q1, q2):
    rows, cols, depth = costs_ref.shape
    count = len(south)

    def both(first, i, v):
        out = []
        for at, part in ((i, v[:count]), (rows - 1 - i, v[count:])):
            best, low = relax(list(part), q1, q2)
            extra = [x - low for x in best]
            if not first:
                extra = [a + b for a, b in zip(extra, split(sums_ref[at]))]
            sums_ref[at] = join(extra)
            out += [a + b for a, b in zip(best, split(tiles_ref[at]))]
        return tuple(out)

    v = lax.fori_loop(0, rows // 2, functools.partial(both, True), tuple(south + north), unroll=2)
    lax.fori_loop(rows // 2, rows, functools.partial(both, False), v, unroll=2)

    ident, mix = identity(cols), interleave(depth)
    batch = 4

    def body(i, carry):
        block = sums_ref[pl.ds(i * batch, batch)].reshape(batch * depth, cols)
        flat = dot(ident, block, TRANSPOSED).astype(jnp.bfloat16)
        for n in range(batch):
            y = i * batch + n
            extra = dot(flat[:, n * depth : (n + 1) * depth], mix, PLAIN)
            base_ref[y] = extra + 4.0 * costs_ref[y].astype(jnp.float32) + 2.0 * q2[:1]
        return carry

    lax.fori_loop(0, rows // batch, body, 0, unroll=2)


def lowered(v):
    low = fold_min(v)
    return [x - low for x in v]


def choose(table, here):
    found = jnp.int32(-1)
    for n, value in enumerate(table):
        found = jnp.where(here == n, jnp.int32(value), found)
    return found


def load_arrival(index, arrivals, held_ref):
    @pl.when(index < 0)
    def _():
        held_ref[...] = jnp.zeros(held_ref.shape, held_ref.dtype)

    for n, ref in enumerate(arrivals):

        @pl.when(index == n)
        def _():
            held_ref[...] = ref[...]


def load_verticals(plan, col_here, row_here, arrivals, held_ref):
    for n in range(2):
        hop = row_here - 1 if n == 0 else plan.rows - 2 - row_here
        source = jnp.int32(-1)
        for j in range(plan.rows - 1):
            found = choose([slots[j] for slots in plan.slots], col_here)
            source = jnp.where(hop == j, found, source)
        load_arrival(source, arrivals, held_ref.at[n])


def among(here, columns):
    hit = here == columns[0]
    for c in columns[1:]:
        hit = hit | (here == c)
    return hit


def stage_kernel(plan, s, names, prices_ref, costs_ref, *refs):
    refs = dict(zip(names, refs))
    arrivals = [refs[f"arrival{n}"] for n in range(s)]
    tiles_ref, turned_ref = refs["tiles"], refs["turned"]
    out_ref, held_ref = refs["sent"], refs["held"]
    rows, cols, depth = costs_ref.shape
    col_here, row_here = lax.axis_index("col"), lax.axis_index("row")
    q1, q2 = penalties(prices_ref)

    if s < plan.cols - 1:

        @pl.when((col_here == s) | (col_here == plan.cols - 1 - s))
        def _():
            west = col_here != s
            if s:
                v = split(arrivals[s - 1][...])
            else:
                v = [jnp.zeros((SUB, cols), jnp.float32)] * (depth // SUB)
            if plan.crossing(s - 1):
                other = split(refs["crossed"][...])
                v = [jnp.where(west, b, a) for a, b in zip(v, other)]
            first = 2 * s < plan.cols
            v = sweep(v, tiles_ref, refs["lows"], refs["sums"], rows, west, first, q1, q2)
            out_ref[...] = join(v)

    turning = plan.turning(s)
    if turning:

        @pl.when(among(col_here, turning))
        def _():
            turn_rows(costs_ref, turned_ref)

    if any(s in slots for slots in plan.slots):
        hops = [slots.index(s) if s in slots else -1 for slots in plan.slots]
        source = [slots[j - 1] if j > 0 else -1 for slots, j in zip(plan.slots, hops)]
        hop = choose(hops, col_here)
        north = row_here == plan.rows - 1 - hop

        @pl.when((hop >= 0) & ((row_here == hop) | north))
        def _():
            load_arrival(choose(source, col_here), arrivals, held_ref.at[0])
            v = descend(split(held_ref[0]), turned_ref, north, q1, q2)
            out_ref[...] = join(lowered(v))

    settling = plan.settling(s)
    if settling:

        @pl.when(among(col_here, settling))
        def _():
            load_verticals(plan, col_here, row_here, arrivals, held_ref)
            south, north = split(held_ref[0]), split(held_ref[1])
            settle(south, north, costs_ref, turned_ref, refs["vsums"], refs["base"], q1, q2)


def skew(v, lane, sub):
    count = len(v)
    bit = 1
    while bit < SUB:
        taken = (lane & bit) != 0
        inner = sub < SUB - bit
        up = [pltpu.roll(a, SUB - bit, 0) for a in v]
        v = [
            jnp.where(taken, jnp.where(inner, up[k], up[(k + 1) % count]), v[k])
            for k in range(count)
        ]
        bit *= 2
    while bit < SUB * count:
        taken = (lane & bit) != 0
        v = [jnp.where(taken, v[(k + bit // SUB) % count], v[k]) for k in range(count)]
        bit *= 2
    return v


def final_kernel(plan, names, prices_ref, costs_ref, *refs):
    refs = dict(zip(names, refs))
    arrivals = [refs[f"arrival{n}"] for n in range(plan.stages)]
    rows, cols, depth = costs_ref.shape
    lanes = cols
    held_ref, sums_ref, base_ref, natural_ref = (
        refs["held"], refs["sums"], refs["base"], refs["natural"]
    )
    q1, q2 = penalties(prices_ref)
    col_here, row_here = lax.axis_index("col"), lax.axis_index("row")

    late = plan.settling(plan.stages)
    if late:

        @pl.when(among(col_here, late))
        def _():
            load_verticals(plan, col_here, row_here, arrivals, held_ref)
            south, north = split(held_ref[0]), split(held_ref[1])
            settle(south, north, costs_ref, refs["turned"], refs["vsums"], base_ref, q1, q2)

    @pl.when((col_here == 0) | (col_here == plan.cols - 1))
    def _():
        v = split(arrivals[plan.cols - 2][...])
        sweep(v, refs["tiles"], refs["lows"], sums_ref, rows, col_here == 0, False, q1, q2)

    order, mix = interleave(2 * cols), interleave(depth)

    def turn(i, carry):
        pair = jnp.concatenate([sums_ref[2 * i], sums_ref[2 * i + 1]], axis=1)
        flat = dot(order, pair, TRANSPOSED).astype(jnp.bfloat16)
        at = pl.ds(pl.multiple_of(i * SUB, SUB), SUB)
        natural_ref[:, at, :] = dot(flat, mix, PLAIN).reshape(rows, SUB, depth)
        return carry

    lax.fori_loop(0, cols // SUB, turn, 0, unroll=4)

    lane = lax.broadcasted_iota(jnp.int32, (SUB, lanes), 1)
    sub = lax.broadcasted_iota(jnp.int32, (SUB, lanes), 0)
    half = rows // 2
    middle = cols // SUB // 2

    def finish(y, carry):
        turned = []
        for at in (y, y + half):
            summed = natural_ref[at] + base_ref[at]
            view = (summed * (1.0 / 64.0)).astype(jnp.bfloat16)
            refs["left"][at] = view
            turned.append(skew(split(view), lane, sub))
            refs["skewed"][at] = join(turned[-1])
        corner = [
            jnp.where(lane >= lanes // 2, a, pltpu.roll(b, lanes // 2, 1))
            for a, b in zip(turned[0][:middle], turned[1][:middle])
        ]
        refs["packed"][y] = join(corner + turned[0][middle:] + turned[1][middle:])
        return carry

    lax.fori_loop(0, half, finish, 0, unroll=2)


def merge_kernel(skewed_ref, packed_ref, right_ref):
    rows, cols, depth = skewed_ref.shape
    lane = lax.broadcasted_iota(jnp.int32, (SUB, depth), 1)
    sub = lax.broadcasted_iota(jnp.int32, (SUB, depth), 0)
    half = rows // 2
    middle = cols // SUB // 2

    def body(y, carry):
        packed = split(packed_ref[y])
        corner = packed[:middle]
        theirs = [
            corner + packed[middle : 2 * middle],
            [pltpu.roll(x, depth // 2, 1) for x in corner] + packed[2 * middle :],
        ]
        for at, other in zip((y, y + half), theirs):
            mine = split(skewed_ref[at])
            right_ref[at] = join(
                [
                    jnp.where(lane + sub + k * SUB < cols, a, b)
                    for k, (a, b) in enumerate(zip(mine, other))
                ]
            )
        return carry

    lax.fori_loop(0, half, body, 0, unroll=2)


class Plan:
    def __init__(self, rows, cols):
        self.rows, self.cols = rows, cols
        self.slots = []
        for c in range(cols):
            busy = {c - 1, c, cols - 2 - c, cols - 1 - c}
            free = [s for s in range(cols + 4 + rows) if s not in busy or s >= cols - 1]
            self.slots.append(free[: rows - 1])
        last = [slots[-1] + 1 for slots in self.slots if slots]
        self.stages = max([cols - 1] + last)

    def crossing(self, s):
        return 2 * s == self.cols - 2

    def numbers(self, pairs):
        number = lambda place: place[0] * self.cols + place[1]
        return [(number(a), number(b)) for a, b in pairs]

    def crossed_route(self, s):
        return self.numbers([((r, s + 1), (r, s)) for r in range(self.rows)])

    def route(self, s):
        pairs = []
        if s < self.cols - 1:
            for r in range(self.rows):
                pairs.append(((r, s), (r, s + 1)))
                if not self.crossing(s):
                    pairs.append(((r, self.cols - 1 - s), (r, self.cols - 2 - s)))
        for c, slots in enumerate(self.slots):
            if s in slots:
                j = slots.index(s)
                pairs += [
                    ((j, c), (j + 1, c)),
                    ((self.rows - 1 - j, c), (self.rows - 2 - j, c)),
                ]
        return self.numbers(pairs)

    def turning(self, s):
        ends = {0, self.cols - 1}
        return [c for c in range(self.cols) if s == (1 if c in ends else 0)]

    def settling(self, s):
        found = []
        for c, slots in enumerate(self.slots):
            at = slots[-1] + 1
            while at < self.stages and at in (c, self.cols - 1 - c):
                at += 1
            if at == s:
                found.append(c)
        return found


def in_vmem(count):
    return [pl.BlockSpec(memory_space=pltpu.VMEM)] * count


def shards(costs, p_small, p_large):
    rows, cols, depth = costs.shape
    plan = Plan(lax.axis_size("row"), lax.axis_size("col"))
    params = {"vmem_limit_bytes": LIMIT}
    front = jax.ShapeDtypeStruct((depth, cols), jnp.bfloat16)
    tile = jax.ShapeDtypeStruct((rows, cols, depth), jnp.bfloat16)
    shapes = {
        "sums": jax.ShapeDtypeStruct((rows, depth, cols), jnp.bfloat16),
        "turned": jax.ShapeDtypeStruct((rows, depth, cols), jnp.bfloat16),
        "base": jax.ShapeDtypeStruct((rows, cols, depth), jnp.float32),
    }
    held = pltpu.VMEM((2, depth, cols), jnp.bfloat16)
    vsums = pltpu.VMEM((rows, depth, cols), jnp.bfloat16)

    tiles, lows, prices, near = pl.pallas_call(
        prepare_kernel,
        out_shape=(
            jax.ShapeDtypeStruct((cols, depth, cols), jnp.float32),
            jax.ShapeDtypeStruct((cols, SUB, cols), jnp.float32),
            jax.ShapeDtypeStruct((2, SUB, cols), jnp.float32),
            tile,
        ),
        in_specs=in_vmem(1) + [pl.BlockSpec(memory_space=pltpu.HBM)] * 2,
        out_specs=tuple(in_vmem(4)),
        scratch_shapes=[
            pltpu.VMEM((cols // SUB, depth, rows * SUB), jnp.bfloat16),
            pltpu.SMEM((2, 1), jnp.int32),
            pltpu.SemaphoreType.DMA((2,)),
        ],
        compiler_params=pltpu.CompilerParams(**params),
        name="prepare",
    )(costs, p_small, p_large)
    buffers = {"tiles": tiles, "lows": lows}

    def run(body, name, results, reads, writes, scratch):
        known = [n for n in writes if n in buffers]
        inputs = reads + known
        outputs = list(results) + writes
        names = [n for n in reads] + [f"{n}_before" for n in known] + outputs + list(scratch)
        lead = 2
        values = pl.pallas_call(
            functools.partial(body, names),
            out_shape=tuple([results[n] for n in results] + [shapes[n] for n in writes]),
            in_specs=in_vmem(lead + len(inputs)),
            out_specs=tuple(in_vmem(len(outputs))),
            scratch_shapes=list(scratch.values()),
            input_output_aliases={
                lead + len(reads) + n: outputs.index(name) for n, name in enumerate(known)
            },
            compiler_params=pltpu.CompilerParams(**params),
            name=name,
        )(prices, near, *[buffers[n] for n in inputs])
        buffers.update(zip(outputs, values))

    for s in range(plan.stages):
        writes = ["sums"] if s < plan.cols - 1 else []
        writes += ["turned"] if s < 2 else []
        writes += ["base"] if plan.settling(s) else []
        reads = ["tiles", "lows"] + ([] if "turned" in writes else ["turned"])
        reads += [f"arrival{n}" for n in range(s)]
        reads += ["crossed"] if plan.crossing(s - 1) else []
        run(
            functools.partial(stage_kernel, plan, s),
            f"stage{s}",
            {"sent": front},
            reads,
            writes,
            {"held": held, "vsums": vsums},
        )
        buffers[f"arrival{s}"] = lax.ppermute(buffers["sent"], ("row", "col"), plan.route(s))
        if plan.crossing(s):
            route = plan.crossed_route(s)
            buffers["crossed"] = lax.ppermute(buffers["sent"], ("row", "col"), route)

    run(
        functools.partial(final_kernel, plan),
        "final",
        {
            "left": tile,
            "skewed": tile,
            "packed": jax.ShapeDtypeStruct((rows // 2, cols // 2 * 3, depth), jnp.bfloat16),
        },
        ["tiles", "lows", "turned"] + [f"arrival{n}" for n in range(plan.stages)],
        ["sums", "base"],
        {
            "held": held,
            "vsums": vsums,
            "natural": pltpu.VMEM((rows, cols, depth), jnp.float32),
        },
    )
    arrived = lax.ppermute(buffers["packed"], "col", [(i, i - 1) for i in range(1, plan.cols)])
    right_view = pl.pallas_call(
        merge_kernel,
        out_shape=tile,
        in_specs=in_vmem(2),
        out_specs=pl.BlockSpec(memory_space=pltpu.VMEM),
        compiler_params=pltpu.CompilerParams(**params),
        name="merge",
    )(buffers["skewed"], arrived)
    return buffers["left"], right_view


def solution(mesh):
    placed = (P("row", "col", None), P(), P())
    return jax.shard_map(
        shards,
        mesh=mesh,
        in_specs=placed,
        out_specs=(P("row", "col", None), P("row", "col", None)),
        check_vma=False,
    )
```

```python
import functools

import jax
import jax.numpy as jnp
from jax import lax
from jax.experimental import pallas as pl
from jax.experimental.pallas import tpu as pltpu
from jax.sharding import PartitionSpec as P

SUB = 8
BIG = 1e30
TRANSPOSED = (((1,), (1,)), ((), ()))
PLAIN = (((1,), (0,)), ((), ()))
LIMIT = 20 * 1024 * 1024


def one_hot(rule, size):
    row = lax.broadcasted_iota(jnp.int32, (size, size), 0)
    col = lax.broadcasted_iota(jnp.int32, (size, size), 1)
    return jnp.where(rule(row, col), 1.0, 0.0).astype(jnp.bfloat16)


def interleave(size):
    return one_hot(lambda r, c: c == (r % SUB) * (size // SUB) + r // SUB, size)


def identity(size):
    return one_hot(lambda r, c: r == c, size)


def dot(a, b, dims):
    return lax.dot_general(a, b, dims, preferred_element_type=jnp.float32)


def split(block):
    wide = block.astype(jnp.float32)
    return [wide[i : i + SUB] for i in range(0, wide.shape[0], SUB)]


def join(parts):
    return jnp.concatenate(parts, axis=0).astype(jnp.bfloat16)


def fold_min(parts):
    parts = list(parts)
    while len(parts) > 1:
        parts = [jnp.minimum(a, b) for a, b in zip(parts[::2], parts[1::2])]
    low = parts[0]
    for shift in (4, 2, 1):
        low = jnp.minimum(low, pltpu.roll(low, shift, 0))
    return low


def relax(v, q1, q2):
    sub = lax.broadcasted_iota(jnp.int32, v[0].shape, 0)
    under = jnp.where(sub == 0, BIG, pltpu.roll(v[-1], 1, 0))
    over = jnp.where(sub == SUB - 1, BIG, pltpu.roll(v[0], SUB - 1, 0))
    low = fold_min(v)
    jump = low + q2
    below = [under] + v[:-1]
    above = v[1:] + [over]
    best = [
        jnp.minimum(jnp.minimum(x, jump), jnp.minimum(a, b) + q1)
        for x, a, b in zip(v, below, above)
    ]
    return best, low


def penalties(prices_ref):
    return prices_ref[0], prices_ref[1]


def spread(rows, lanes, first):
    row = lax.broadcasted_iota(jnp.int32, (rows * SUB, 2 * lanes), 0)
    col = lax.broadcasted_iota(jnp.int32, (rows * SUB, 2 * lanes), 1)
    hit = row == (col % lanes % rows) * SUB + first + col // lanes
    return jnp.where(hit, 1.0, 0.0).astype(jnp.bfloat16)


def prepare_kernel(
    costs_ref, small_ref, large_ref,
    out_ref, low_ref, prices_ref, near_ref,
    mixed_ref, price_refs, arrived,
):
    rows, cols, depth = costs_ref.shape
    mix = interleave(depth)
    fetches = [
        pltpu.make_async_copy(ref, price_refs.at[n], arrived.at[n])
        for n, ref in enumerate((small_ref, large_ref))
    ]
    for fetch in fetches:
        fetch.start()

    def mixed(i, carry):
        at = pl.ds(pl.multiple_of(i * 2 * SUB, 2 * SUB), 2 * SUB)
        block = costs_ref[:, at, :]
        near_ref[:, at, :] = block
        wide = block.astype(jnp.float32)
        for n in range(2):
            part = wide[:, n * SUB : (n + 1) * SUB].reshape(rows * SUB, depth)
            flat = dot(mix, part.astype(jnp.bfloat16), TRANSPOSED)
            mixed_ref[2 * i + n] = flat.astype(jnp.bfloat16)
        return carry

    lax.fori_loop(0, cols // SUB // 2, mixed, 0, unroll=2)
    for j in range(0, SUB, 2):
        pick = spread(rows, cols, j)

        def body(i, carry):
            flat = dot(mixed_ref[i], pick, PLAIN)
            for n in range(2):
                part = flat[:, n * cols : (n + 1) * cols]
                out_ref[i * SUB + j + n] = part
                low_ref[i * SUB + j + n] = fold_min(split(part))
            return carry

        lax.fori_loop(0, cols // SUB, body, 0, unroll=4)

    for n, fetch in enumerate(fetches):
        fetch.wait()
        price = jnp.full(prices_ref.shape[1:], price_refs[n, 0], jnp.int32)
        prices_ref[n] = price.astype(jnp.float32)


def turn_rows(costs_ref, tiles_ref):
    rows, cols, depth = costs_ref.shape
    mix = interleave(depth)
    batch = 4

    def body(i, carry):
        block = costs_ref[pl.ds(i * batch, batch)].reshape(batch * cols, depth)
        flat = dot(mix, block, TRANSPOSED).astype(jnp.bfloat16)
        for n in range(batch):
            tiles_ref[i * batch + n] = flat[:, n * cols : (n + 1) * cols]
        return carry

    lax.fori_loop(0, rows // batch, body, 0, unroll=2)


def sweep(v, tiles_ref, lows_ref, raw_ref, jumps_ref, rows, west, q1, q2):
    cols, depth, lanes = tiles_ref.shape
    pack = lanes // rows
    lane = lax.broadcasted_iota(jnp.int32, (SUB, lanes), 1)
    sub = lax.broadcasted_iota(jnp.int32, (SUB, lanes), 0)
    groups = [jnp.where(west, pack - 1 - j, j) for j in range(pack)]
    mine = [(lane >= g * rows) & (lane < (g + 1) * rows) for g in groups]

    def body(i, carry):
        v, jump = list(carry[:-1]), carry[-1]
        at = jnp.where(west, cols // pack - 1 - i, i)
        for j in range(pack):
            x = at * pack + groups[j]
            c = split(tiles_ref[x])
            below = [jnp.where(sub == 0, BIG, pltpu.roll(v[-1], 1, 0))] + v[:-1]
            above = v[1:] + [jnp.where(sub == SUB - 1, BIG, pltpu.roll(v[0], SUB - 1, 0))]
            near = [
                jnp.minimum(n, jnp.minimum(a, b) + q1) for n, a, b in zip(v, below, above)
            ]
            best = [jnp.minimum(n, jump) for n in near]
            for k, x_best in enumerate(best):
                pltpu.store(raw_ref.at[at, pl.ds(k * SUB, SUB), :], x_best, mask=mine[j])
            pltpu.store(jumps_ref.at[at], jump, mask=mine[j])
            low = fold_min([n + k for n, k in zip(near, c)])
            v = [n + k for n, k in zip(best, c)]
            jump = jnp.minimum(low, lows_ref[x] + jump) + q2
        return tuple(v) + (jump,)

    last = lax.fori_loop(0, cols // pack, body, tuple(v) + (fold_min(v) + q2,))
    low = last[-1] - q2
    return [x - low for x in last[:-1]]


def descend(v, tiles_ref, north, q1, q2):
    rows = tiles_ref.shape[0]

    def body(i, v):
        best, _ = relax(list(v), q1, q2)
        at = jnp.where(north, rows - 1 - i, i)
        return tuple(a + b for a, b in zip(best, split(tiles_ref[at])))

    return list(lax.fori_loop(0, rows, body, tuple(v), unroll=4))


def settle(south, north, costs_ref, tiles_ref, sums_ref, base_ref, q1, q2):
    rows, cols, depth = costs_ref.shape
    count = len(south)

    def both(first, i, v):
        out = []
        for at, part in ((i, v[:count]), (rows - 1 - i, v[count:])):
            best, low = relax(list(part), q1, q2)
            extra = [x - low for x in best]
            if not first:
                extra = [a + b for a, b in zip(extra, split(sums_ref[at]))]
            sums_ref[at] = join(extra)
            out += [a + b for a, b in zip(best, split(tiles_ref[at]))]
        return tuple(out)

    v = lax.fori_loop(0, rows // 2, functools.partial(both, True), tuple(south + north), unroll=2)
    lax.fori_loop(rows // 2, rows, functools.partial(both, False), v, unroll=2)

    ident, mix = identity(cols), interleave(depth)
    batch = 4

    def body(i, carry):
        block = sums_ref[pl.ds(i * batch, batch)].reshape(batch * depth, cols)
        flat = dot(ident, block, TRANSPOSED).astype(jnp.bfloat16)
        for n in range(batch):
            y = i * batch + n
            extra = dot(flat[:, n * depth : (n + 1) * depth], mix, PLAIN)
            base_ref[y] = extra + 4.0 * costs_ref[y].astype(jnp.float32) + 2.0 * q2[:1]
        return carry

    lax.fori_loop(0, rows // batch, body, 0, unroll=2)


def lowered(v):
    low = fold_min(v)
    return [x - low for x in v]


def choose(table, here):
    found = jnp.int32(-1)
    for n, value in enumerate(table):
        found = jnp.where(here == n, jnp.int32(value), found)
    return found


def load_arrival(index, arrivals, held_ref):
    @pl.when(index < 0)
    def _():
        held_ref[...] = jnp.zeros(held_ref.shape, held_ref.dtype)

    for n, ref in enumerate(arrivals):

        @pl.when(index == n)
        def _():
            held_ref[...] = ref[...]


def load_verticals(plan, col_here, row_here, arrivals, held_ref):
    for n in range(2):
        hop = row_here - 1 if n == 0 else plan.rows - 2 - row_here
        source = jnp.int32(-1)
        for j in range(plan.rows - 1):
            found = choose([slots[j] for slots in plan.slots], col_here)
            source = jnp.where(hop == j, found, source)
        load_arrival(source, arrivals, held_ref.at[n])


def among(here, columns):
    hit = here == columns[0]
    for c in columns[1:]:
        hit = hit | (here == c)
    return hit


def stage_kernel(plan, s, names, prices_ref, costs_ref, *refs):
    refs = dict(zip(names, refs))
    arrivals = [refs[f"arrival{n}"] for n in range(s)]
    tiles_ref, turned_ref = refs["tiles"], refs["turned"]
    out_ref, held_ref = refs["sent"], refs["held"]
    rows, cols, depth = costs_ref.shape
    col_here, row_here = lax.axis_index("col"), lax.axis_index("row")
    q1, q2 = penalties(prices_ref)

    hop = plan.hop_at(s)
    if hop is None:
        out_ref[...] = refs["passed"][...]
    elif hop < plan.cols - 1:

        @pl.when((col_here == hop) | (col_here == plan.cols - 1 - hop))
        def _():
            west = col_here != hop
            if hop:
                v = split(arrivals[plan.step(hop - 1, False)][...])
                other = split(arrivals[plan.step(hop - 1, True)][...])
                v = [jnp.where(west, b, a) for a, b in zip(v, other)]
            else:
                v = [jnp.zeros((SUB, cols), jnp.float32)] * (depth // SUB)
            raw, jumps = (refs[n] for n in plan.paths(hop))
            out_ref[...] = join(sweep(v, tiles_ref, refs["lows"], raw, jumps, rows, west, q1, q2))

    turning = plan.turning(s)
    if turning:

        @pl.when(among(col_here, turning))
        def _():
            turn_rows(costs_ref, turned_ref)

    if any(s in slots for slots in plan.slots):
        hops = [slots.index(s) if s in slots else -1 for slots in plan.slots]
        source = [slots[j - 1] if j > 0 else -1 for slots, j in zip(plan.slots, hops)]
        hop = choose(hops, col_here)
        north = row_here == plan.rows - 1 - hop

        @pl.when((hop >= 0) & ((row_here == hop) | north))
        def _():
            load_arrival(choose(source, col_here), arrivals, held_ref.at[0])
            v = descend(split(held_ref[0]), turned_ref, north, q1, q2)
            out_ref[...] = join(lowered(v))

    settling = plan.settling(s)
    if settling:

        @pl.when(among(col_here, settling))
        def _():
            load_verticals(plan, col_here, row_here, arrivals, held_ref)
            south, north = split(held_ref[0]), split(held_ref[1])
            settle(south, north, costs_ref, turned_ref, refs["vsums"], refs["base"], q1, q2)


def skew(v, lane, sub):
    count = len(v)
    bit = 1
    while bit < SUB:
        taken = (lane & bit) != 0
        inner = sub < SUB - bit
        up = [pltpu.roll(a, SUB - bit, 0) for a in v]
        v = [
            jnp.where(taken, jnp.where(inner, up[k], up[(k + 1) % count]), v[k])
            for k in range(count)
        ]
        bit *= 2
    while bit < SUB * count:
        taken = (lane & bit) != 0
        v = [jnp.where(taken, v[(k + bit // SUB) % count], v[k]) for k in range(count)]
        bit *= 2
    return v


def final_kernel(plan, names, prices_ref, costs_ref, *refs):
    refs = dict(zip(names, refs))
    arrivals = [refs[f"arrival{n}"] for n in range(plan.stages)]
    rows, cols, depth = costs_ref.shape
    lanes = cols
    held_ref, base_ref, natural_ref = refs["held"], refs["base"], refs["natural"]
    q1, q2 = penalties(prices_ref)
    col_here, row_here = lax.axis_index("col"), lax.axis_index("row")

    late = plan.settling(plan.stages)
    if late:

        @pl.when(among(col_here, late))
        def _():
            load_verticals(plan, col_here, row_here, arrivals, held_ref)
            south, north = split(held_ref[0]), split(held_ref[1])
            settle(south, north, costs_ref, refs["turned"], refs["vsums"], base_ref, q1, q2)

    @pl.when((col_here == 0) | (col_here == plan.cols - 1))
    def _():
        v = split(arrivals[plan.step(plan.cols - 2, True)][...])
        raw, jumps = refs["second"], refs["second_jumps"]
        sweep(v, refs["tiles"], refs["lows"], raw, jumps, rows, col_here == 0, q1, q2)

    order, mix = interleave(2 * cols), interleave(depth)

    def added(at):
        total = None
        for name in ("first", "second"):
            jump = refs[f"{name}_jumps"][at]
            part = [x - jump for x in split(refs[name][at])]
            total = part if total is None else [a + b for a, b in zip(total, part)]
        return join(total)

    def turn(i, carry):
        pair = jnp.concatenate([added(2 * i), added(2 * i + 1)], axis=1)
        flat = dot(order, pair, TRANSPOSED).astype(jnp.bfloat16)
        at = pl.ds(pl.multiple_of(i * SUB, SUB), SUB)
        natural_ref[:, at, :] = dot(flat, mix, PLAIN).reshape(rows, SUB, depth)
        return carry

    lax.fori_loop(0, cols // SUB, turn, 0, unroll=4)

    lane = lax.broadcasted_iota(jnp.int32, (SUB, lanes), 1)
    sub = lax.broadcasted_iota(jnp.int32, (SUB, lanes), 0)
    half = rows // 2
    middle = cols // SUB // 2

    def finish(y, carry):
        turned = []
        for at in (y, y + half):
            summed = natural_ref[at] + base_ref[at]
            view = (summed * (1.0 / 64.0)).astype(jnp.bfloat16)
            refs["left"][at] = view
            turned.append(skew(split(view), lane, sub))
            refs["skewed"][at] = join(turned[-1])
        corner = [
            jnp.where(lane >= lanes // 2, a, pltpu.roll(b, lanes // 2, 1))
            for a, b in zip(turned[0][:middle], turned[1][:middle])
        ]
        refs["packed"][y] = join(corner + turned[0][middle:] + turned[1][middle:])
        return carry

    lax.fori_loop(0, half, finish, 0, unroll=2)


def merge_kernel(skewed_ref, packed_ref, right_ref):
    rows, cols, depth = skewed_ref.shape
    lane = lax.broadcasted_iota(jnp.int32, (SUB, depth), 1)
    sub = lax.broadcasted_iota(jnp.int32, (SUB, depth), 0)
    half = rows // 2
    middle = cols // SUB // 2

    def body(y, carry):
        packed = split(packed_ref[y])
        corner = packed[:middle]
        theirs = [
            corner + packed[middle : 2 * middle],
            [pltpu.roll(x, depth // 2, 1) for x in corner] + packed[2 * middle :],
        ]
        for at, other in zip((y, y + half), theirs):
            mine = split(skewed_ref[at])
            right_ref[at] = join(
                [
                    jnp.where(lane + sub + k * SUB < cols, a, b)
                    for k, (a, b) in enumerate(zip(mine, other))
                ]
            )
        return carry

    lax.fori_loop(0, half, body, 0, unroll=2)


class Plan:
    def __init__(self, rows, cols):
        self.rows, self.cols = rows, cols
        self.half = cols // 2
        self.slots = []
        for c in range(cols):
            busy = set()
            if c > 0:
                busy |= {self.step(c - 1, False), self.step(cols - 1 - c, True)}
            if c < cols - 1:
                busy |= {self.step(c, False), self.step(cols - 2 - c, True)}
            free = [s for s in range(cols + 4 + rows) if s not in busy]
            self.slots.append(free[: rows - 1])
        last = [slots[-1] + 1 for slots in self.slots if slots]
        self.stages = max([cols] + last)

    def step(self, hop, west):
        if hop < self.half - 1:
            return hop
        if hop == self.half - 1:
            return hop + 1 if west else hop
        return hop + 1

    def hop_at(self, s):
        if s == self.half:
            return None
        return s if s < self.half else s - 1

    def paths(self, hop):
        name = "first" if hop < self.half else "second"
        return [name, f"{name}_jumps"]

    def route(self, s):
        pairs = []
        for h in range(self.cols - 1):
            for r in range(self.rows):
                if self.step(h, False) == s:
                    pairs.append(((r, h), (r, h + 1)))
                if self.step(h, True) == s:
                    pairs.append(((r, self.cols - 1 - h), (r, self.cols - 2 - h)))
        for c, slots in enumerate(self.slots):
            if s in slots:
                j = slots.index(s)
                pairs += [
                    ((j, c), (j + 1, c)),
                    ((self.rows - 1 - j, c), (self.rows - 2 - j, c)),
                ]
        number = lambda place: place[0] * self.cols + place[1]
        return [(number(a), number(b)) for a, b in pairs]

    def turning(self, s):
        ends = {0, self.cols - 1}
        return [c for c in range(self.cols) if s == (1 if c in ends else 0)]

    def settling(self, s):
        found = []
        for c, slots in enumerate(self.slots):
            at = slots[-1] + 1
            while at < self.stages and self.hop_at(at) in (c, self.cols - 1 - c):
                at += 1
            if at == s:
                found.append(c)
        return found


def in_vmem(count):
    return [pl.BlockSpec(memory_space=pltpu.VMEM)] * count


def shards(costs, p_small, p_large):
    rows, cols, depth = costs.shape
    plan = Plan(lax.axis_size("row"), lax.axis_size("col"))
    params = {"vmem_limit_bytes": LIMIT}
    front = jax.ShapeDtypeStruct((depth, cols), jnp.bfloat16)
    tile = jax.ShapeDtypeStruct((rows, cols, depth), jnp.bfloat16)
    shapes = {
        "first": jax.ShapeDtypeStruct((rows, depth, cols), jnp.float32),
        "first_jumps": jax.ShapeDtypeStruct((rows, SUB, cols), jnp.float32),
        "second": jax.ShapeDtypeStruct((rows, depth, cols), jnp.float32),
        "second_jumps": jax.ShapeDtypeStruct((rows, SUB, cols), jnp.float32),
        "turned": jax.ShapeDtypeStruct((rows, depth, cols), jnp.bfloat16),
        "base": jax.ShapeDtypeStruct((rows, cols, depth), jnp.float32),
    }
    held = pltpu.VMEM((2, depth, cols), jnp.bfloat16)
    vsums = pltpu.VMEM((rows, depth, cols), jnp.bfloat16)

    tiles, lows, prices, near = pl.pallas_call(
        prepare_kernel,
        out_shape=(
            jax.ShapeDtypeStruct((cols, depth, cols), jnp.float32),
            jax.ShapeDtypeStruct((cols, SUB, cols), jnp.float32),
            jax.ShapeDtypeStruct((2, SUB, cols), jnp.float32),
            tile,
        ),
        in_specs=in_vmem(1) + [pl.BlockSpec(memory_space=pltpu.HBM)] * 2,
        out_specs=tuple(in_vmem(4)),
        scratch_shapes=[
            pltpu.VMEM((cols // SUB, depth, rows * SUB), jnp.bfloat16),
            pltpu.SMEM((2, 1), jnp.int32),
            pltpu.SemaphoreType.DMA((2,)),
        ],
        compiler_params=pltpu.CompilerParams(**params),
        name="prepare",
    )(costs, p_small, p_large)
    buffers = {"tiles": tiles, "lows": lows}

    def run(body, name, results, reads, writes, scratch):
        known = [n for n in writes if n in buffers]
        inputs = reads + known
        outputs = list(results) + writes
        names = [n for n in reads] + [f"{n}_before" for n in known] + outputs + list(scratch)
        lead = 2
        values = pl.pallas_call(
            functools.partial(body, names),
            out_shape=tuple([results[n] for n in results] + [shapes[n] for n in writes]),
            in_specs=in_vmem(lead + len(inputs)),
            out_specs=tuple(in_vmem(len(outputs))),
            scratch_shapes=list(scratch.values()),
            input_output_aliases={
                lead + len(reads) + n: outputs.index(name) for n, name in enumerate(known)
            },
            compiler_params=pltpu.CompilerParams(**params),
            name=name,
        )(prices, near, *[buffers[n] for n in inputs])
        buffers.update(zip(outputs, values))

    for s in range(plan.stages):
        hop = plan.hop_at(s)
        writes = plan.paths(hop) if hop is not None and hop < plan.cols - 1 else []
        writes += ["turned"] if s < 2 else []
        writes += ["base"] if plan.settling(s) else []
        reads = ["tiles", "lows"] + ([] if "turned" in writes else ["turned"])
        reads += [f"arrival{n}" for n in range(s)]
        reads += ["passed"] if hop is None else []
        run(
            functools.partial(stage_kernel, plan, s),
            f"stage{s}",
            {"sent": front},
            reads,
            writes,
            {"held": held, "vsums": vsums},
        )
        buffers[f"arrival{s}"] = lax.ppermute(buffers["sent"], ("row", "col"), plan.route(s))
        buffers["passed"] = buffers["sent"]

    run(
        functools.partial(final_kernel, plan),
        "final",
        {
            "left": tile,
            "skewed": tile,
            "packed": jax.ShapeDtypeStruct((rows // 2, cols // 2 * 3, depth), jnp.bfloat16),
        },
        ["tiles", "lows", "turned", "first", "first_jumps"]
        + [f"arrival{n}" for n in range(plan.stages)],
        ["second", "second_jumps", "base"],
        {
            "held": held,
            "vsums": vsums,
            "natural": pltpu.VMEM((rows, cols, depth), jnp.float32),
        },
    )
    arrived = lax.ppermute(buffers["packed"], "col", [(i, i - 1) for i in range(1, plan.cols)])
    right_view = pl.pallas_call(
        merge_kernel,
        out_shape=tile,
        in_specs=in_vmem(2),
        out_specs=pl.BlockSpec(memory_space=pltpu.VMEM),
        compiler_params=pltpu.CompilerParams(**params),
        name="merge",
    )(buffers["skewed"], arrived)
    return buffers["left"], right_view


def solution(mesh):
    placed = (P("row", "col", None), P(), P())
    return jax.shard_map(
        shards,
        mesh=mesh,
        in_specs=placed,
        out_specs=(P("row", "col", None), P("row", "col", None)),
        check_vma=False,
    )
```

```python
import functools

import jax
import jax.numpy as jnp
from jax import lax
from jax.experimental import pallas as pl
from jax.experimental.pallas import tpu as pltpu
from jax.sharding import PartitionSpec as P

SUB = 8
BIG = 1e30
TRANSPOSED = (((1,), (1,)), ((), ()))
PLAIN = (((1,), (0,)), ((), ()))
LIMIT = 20 * 1024 * 1024


def one_hot(rule, size):
    row = lax.broadcasted_iota(jnp.int32, (size, size), 0)
    col = lax.broadcasted_iota(jnp.int32, (size, size), 1)
    return jnp.where(rule(row, col), 1.0, 0.0).astype(jnp.bfloat16)


def interleave(size):
    return one_hot(lambda r, c: c == (r % SUB) * (size // SUB) + r // SUB, size)


def identity(size):
    return one_hot(lambda r, c: r == c, size)


def dot(a, b, dims):
    return lax.dot_general(a, b, dims, preferred_element_type=jnp.float32)


def split(block):
    wide = block.astype(jnp.float32)
    return [wide[i : i + SUB] for i in range(0, wide.shape[0], SUB)]


def join(parts):
    return jnp.concatenate(parts, axis=0).astype(jnp.bfloat16)


def fold_min(parts):
    parts = list(parts)
    while len(parts) > 1:
        parts = [jnp.minimum(a, b) for a, b in zip(parts[::2], parts[1::2])]
    low = parts[0]
    for shift in (4, 2, 1):
        low = jnp.minimum(low, pltpu.roll(low, shift, 0))
    return low


def relax(v, q1, q2):
    sub = lax.broadcasted_iota(jnp.int32, v[0].shape, 0)
    under = jnp.where(sub == 0, BIG, pltpu.roll(v[-1], 1, 0))
    over = jnp.where(sub == SUB - 1, BIG, pltpu.roll(v[0], SUB - 1, 0))
    low = fold_min(v)
    jump = low + q2
    below = [under] + v[:-1]
    above = v[1:] + [over]
    best = [
        jnp.minimum(jnp.minimum(x, jump), jnp.minimum(a, b) + q1)
        for x, a, b in zip(v, below, above)
    ]
    return best, low


def penalties(prices_ref):
    return prices_ref[0], prices_ref[1]


def spread(rows, lanes, first):
    row = lax.broadcasted_iota(jnp.int32, (rows * SUB, 2 * lanes), 0)
    col = lax.broadcasted_iota(jnp.int32, (rows * SUB, 2 * lanes), 1)
    hit = row == (col % lanes % rows) * SUB + first + col // lanes
    return jnp.where(hit, 1.0, 0.0).astype(jnp.bfloat16)


def prepare_kernel(
    costs_ref, small_ref, large_ref,
    out_ref, low_ref, prices_ref, near_ref,
    mixed_ref, price_refs, arrived,
):
    rows, cols, depth = costs_ref.shape
    mix = interleave(depth)
    fetches = [
        pltpu.make_async_copy(ref, price_refs.at[n], arrived.at[n])
        for n, ref in enumerate((small_ref, large_ref))
    ]
    for fetch in fetches:
        fetch.start()

    def mixed(i, carry):
        at = pl.ds(pl.multiple_of(i * 2 * SUB, 2 * SUB), 2 * SUB)
        block = costs_ref[:, at, :]
        near_ref[:, at, :] = block
        wide = block.astype(jnp.float32)
        for n in range(2):
            part = wide[:, n * SUB : (n + 1) * SUB].reshape(rows * SUB, depth)
            flat = dot(mix, part.astype(jnp.bfloat16), TRANSPOSED)
            mixed_ref[2 * i + n] = flat.astype(jnp.bfloat16)
        return carry

    lax.fori_loop(0, cols // SUB // 2, mixed, 0, unroll=2)
    for j in range(0, SUB, 2):
        pick = spread(rows, cols, j)

        def body(i, carry):
            flat = dot(mixed_ref[i], pick, PLAIN)
            for n in range(2):
                part = flat[:, n * cols : (n + 1) * cols]
                out_ref[i * SUB + j + n] = part
                low_ref[i * SUB + j + n] = fold_min(split(part))
            return carry

        lax.fori_loop(0, cols // SUB, body, 0, unroll=4)

    for n, fetch in enumerate(fetches):
        fetch.wait()
        price = jnp.full(prices_ref.shape[1:], price_refs[n, 0], jnp.int32)
        prices_ref[n] = price.astype(jnp.float32)


def turn_rows(costs_ref, tiles_ref):
    rows, cols, depth = costs_ref.shape
    mix = interleave(depth)
    batch = 4

    def body(i, carry):
        block = costs_ref[pl.ds(i * batch, batch)].reshape(batch * cols, depth)
        flat = dot(mix, block, TRANSPOSED).astype(jnp.bfloat16)
        for n in range(batch):
            tiles_ref[i * batch + n] = flat[:, n * cols : (n + 1) * cols]
        return carry

    lax.fori_loop(0, rows // batch, body, 0, unroll=2)


def sweep(v, tiles_ref, lows_ref, raw_ref, jumps_ref, rows, west, q1, q2):
    cols, depth, lanes = tiles_ref.shape
    pack = lanes // rows
    lane = lax.broadcasted_iota(jnp.int32, (SUB, lanes), 1)
    sub = lax.broadcasted_iota(jnp.int32, (SUB, lanes), 0)
    groups = [jnp.where(west, pack - 1 - j, j) for j in range(pack)]
    mine = [(lane >= g * rows) & (lane < (g + 1) * rows) for g in groups]

    def body(i, carry):
        v, jump = list(carry[:-1]), carry[-1]
        at = jnp.where(west, cols // pack - 1 - i, i)
        for j in range(pack):
            x = at * pack + groups[j]
            c = split(tiles_ref[x])
            below = [jnp.where(sub == 0, BIG, pltpu.roll(v[-1], 1, 0))] + v[:-1]
            above = v[1:] + [jnp.where(sub == SUB - 1, BIG, pltpu.roll(v[0], SUB - 1, 0))]
            near = [
                jnp.minimum(n, jnp.minimum(a, b) + q1) for n, a, b in zip(v, below, above)
            ]
            best = [jnp.minimum(n, jump) for n in near]
            for k, x_best in enumerate(best):
                pltpu.store(raw_ref.at[at, pl.ds(k * SUB, SUB), :], x_best, mask=mine[j])
            pltpu.store(jumps_ref.at[at], jump, mask=mine[j])
            low = fold_min([n + k for n, k in zip(near, c)])
            v = [n + k for n, k in zip(best, c)]
            jump = jnp.minimum(low, lows_ref[x] + jump) + q2
        return tuple(v) + (jump,)

    last = lax.fori_loop(0, cols // pack, body, tuple(v) + (fold_min(v) + q2,))
    low = last[-1] - q2
    return [x - low for x in last[:-1]]


def descend(v, tiles_ref, north, q1, q2):
    rows = tiles_ref.shape[0]

    def body(i, v):
        best, _ = relax(list(v), q1, q2)
        at = jnp.where(north, rows - 1 - i, i)
        return tuple(a + b for a, b in zip(best, split(tiles_ref[at])))

    return list(lax.fori_loop(0, rows, body, tuple(v), unroll=4))


def settle(south, north, costs_ref, tiles_ref, sums_ref, base_ref, q1, q2):
    rows, cols, depth = costs_ref.shape
    count = len(south)

    def both(first, i, v):
        out = []
        for at, part in ((i, v[:count]), (rows - 1 - i, v[count:])):
            best, low = relax(list(part), q1, q2)
            extra = [x - low for x in best]
            if not first:
                extra = [a + b for a, b in zip(extra, split(sums_ref[at]))]
            sums_ref[at] = join(extra)
            out += [a + b for a, b in zip(best, split(tiles_ref[at]))]
        return tuple(out)

    v = lax.fori_loop(0, rows // 2, functools.partial(both, True), tuple(south + north), unroll=2)
    lax.fori_loop(rows // 2, rows, functools.partial(both, False), v, unroll=2)

    ident, mix = identity(cols), interleave(depth)
    batch = 4

    def body(i, carry):
        block = sums_ref[pl.ds(i * batch, batch)].reshape(batch * depth, cols)
        flat = dot(ident, block, TRANSPOSED).astype(jnp.bfloat16)
        for n in range(batch):
            y = i * batch + n
            extra = dot(flat[:, n * depth : (n + 1) * depth], mix, PLAIN)
            base_ref[y] = extra + 4.0 * costs_ref[y].astype(jnp.float32) + 2.0 * q2[:1]
        return carry

    lax.fori_loop(0, rows // batch, body, 0, unroll=2)


def lowered(v):
    low = fold_min(v)
    return [x - low for x in v]


def choose(table, here):
    found = jnp.int32(-1)
    for n, value in enumerate(table):
        found = jnp.where(here == n, jnp.int32(value), found)
    return found


def load_arrival(index, arrivals, held_ref):
    @pl.when(index < 0)
    def _():
        held_ref[...] = jnp.zeros(held_ref.shape, held_ref.dtype)

    for n, ref in enumerate(arrivals):

        @pl.when(index == n)
        def _():
            held_ref[...] = ref[...]


def load_verticals(plan, col_here, row_here, arrivals, held_ref):
    for n in range(2):
        hop = row_here - 1 if n == 0 else plan.rows - 2 - row_here
        source = jnp.int32(-1)
        for j in range(plan.rows - 1):
            found = choose([slots[j] for slots in plan.slots], col_here)
            source = jnp.where(hop == j, found, source)
        load_arrival(source, arrivals, held_ref.at[n])


def among(here, columns):
    hit = here == columns[0]
    for c in columns[1:]:
        hit = hit | (here == c)
    return hit


def stage_kernel(plan, s, names, prices_ref, costs_ref, *refs):
    refs = dict(zip(names, refs))
    arrivals = [refs[f"arrival{n}"] for n in range(s)]
    tiles_ref, turned_ref = refs["tiles"], refs["turned"]
    out_ref, held_ref = refs["sent"], refs["held"]
    rows, cols, depth = costs_ref.shape
    col_here, row_here = lax.axis_index("col"), lax.axis_index("row")
    q1, q2 = penalties(prices_ref)

    hop = plan.hop_at(s)
    if hop is not None and hop < plan.cols - 1:

        @pl.when((col_here == hop) | (col_here == plan.cols - 1 - hop))
        def _():
            west = col_here != hop
            if hop:
                v = split(arrivals[plan.step(hop - 1)][...])
                if hop == plan.half:
                    other = split(refs["crossed"][...])
                    v = [jnp.where(west, b, a) for a, b in zip(v, other)]
            else:
                v = [jnp.zeros((SUB, cols), jnp.float32)] * (depth // SUB)
            raw, jumps = (refs[n] for n in plan.paths(hop))
            out_ref[...] = join(sweep(v, tiles_ref, refs["lows"], raw, jumps, rows, west, q1, q2))

    turning = plan.turning(s)
    if turning:

        @pl.when(among(col_here, turning))
        def _():
            turn_rows(costs_ref, turned_ref)

    if any(s in slots for slots in plan.slots):
        hops = [slots.index(s) if s in slots else -1 for slots in plan.slots]
        source = [slots[j - 1] if j > 0 else -1 for slots, j in zip(plan.slots, hops)]
        hop = choose(hops, col_here)
        north = row_here == plan.rows - 1 - hop

        @pl.when((hop >= 0) & ((row_here == hop) | north))
        def _():
            load_arrival(choose(source, col_here), arrivals, held_ref.at[0])
            v = descend(split(held_ref[0]), turned_ref, north, q1, q2)
            out_ref[...] = join(lowered(v))

    settling = plan.settling(s)
    if settling:

        @pl.when(among(col_here, settling))
        def _():
            load_verticals(plan, col_here, row_here, arrivals, held_ref)
            south, north = split(held_ref[0]), split(held_ref[1])
            settle(south, north, costs_ref, turned_ref, refs["vsums"], refs["base"], q1, q2)


def skew(v, lane, sub):
    count = len(v)
    bit = 1
    while bit < SUB:
        taken = (lane & bit) != 0
        inner = sub < SUB - bit
        up = [pltpu.roll(a, SUB - bit, 0) for a in v]
        v = [
            jnp.where(taken, jnp.where(inner, up[k], up[(k + 1) % count]), v[k])
            for k in range(count)
        ]
        bit *= 2
    while bit < SUB * count:
        taken = (lane & bit) != 0
        v = [jnp.where(taken, v[(k + bit // SUB) % count], v[k]) for k in range(count)]
        bit *= 2
    return v


def final_kernel(plan, names, prices_ref, costs_ref, *refs):
    refs = dict(zip(names, refs))
    arrivals = [refs[f"arrival{n}"] for n in range(plan.stages)]
    rows, cols, depth = costs_ref.shape
    lanes = cols
    held_ref, base_ref, natural_ref = refs["held"], refs["base"], refs["natural"]
    q1, q2 = penalties(prices_ref)
    col_here, row_here = lax.axis_index("col"), lax.axis_index("row")

    late = plan.settling(plan.stages)
    if late:

        @pl.when(among(col_here, late))
        def _():
            load_verticals(plan, col_here, row_here, arrivals, held_ref)
            south, north = split(held_ref[0]), split(held_ref[1])
            settle(south, north, costs_ref, refs["turned"], refs["vsums"], base_ref, q1, q2)

    @pl.when((col_here == 0) | (col_here == plan.cols - 1))
    def _():
        v = split(arrivals[plan.step(plan.cols - 2)][...])
        raw, jumps = refs["second"], refs["second_jumps"]
        sweep(v, refs["tiles"], refs["lows"], raw, jumps, rows, col_here == 0, q1, q2)

    order, mix = interleave(2 * cols), interleave(depth)

    def added(at):
        total = None
        for name in ("first", "second"):
            jump = refs[f"{name}_jumps"][at]
            part = [x - jump for x in split(refs[name][at])]
            total = part if total is None else [a + b for a, b in zip(total, part)]
        return join(total)

    def turn(i, carry):
        pair = jnp.concatenate([added(2 * i), added(2 * i + 1)], axis=1)
        flat = dot(order, pair, TRANSPOSED).astype(jnp.bfloat16)
        at = pl.ds(pl.multiple_of(i * SUB, SUB), SUB)
        natural_ref[:, at, :] = dot(flat, mix, PLAIN).reshape(rows, SUB, depth)
        return carry

    lax.fori_loop(0, cols // SUB, turn, 0, unroll=4)

    lane = lax.broadcasted_iota(jnp.int32, (SUB, lanes), 1)
    sub = lax.broadcasted_iota(jnp.int32, (SUB, lanes), 0)
    half = rows // 2
    middle = cols // SUB // 2

    def finish(y, carry):
        turned = []
        for at in (y, y + half):
            summed = natural_ref[at] + base_ref[at]
            view = (summed * (1.0 / 64.0)).astype(jnp.bfloat16)
            refs["left"][at] = view
            turned.append(skew(split(view), lane, sub))
            refs["skewed"][at] = join(turned[-1])
        corner = [
            jnp.where(lane >= lanes // 2, a, pltpu.roll(b, lanes // 2, 1))
            for a, b in zip(turned[0][:middle], turned[1][:middle])
        ]
        refs["packed"][y] = join(corner + turned[0][middle:] + turned[1][middle:])
        return carry

    lax.fori_loop(0, half, finish, 0, unroll=2)


def merge_kernel(skewed_ref, packed_ref, right_ref):
    rows, cols, depth = skewed_ref.shape
    lane = lax.broadcasted_iota(jnp.int32, (SUB, depth), 1)
    sub = lax.broadcasted_iota(jnp.int32, (SUB, depth), 0)
    half = rows // 2
    middle = cols // SUB // 2

    def body(y, carry):
        packed = split(packed_ref[y])
        corner = packed[:middle]
        theirs = [
            corner + packed[middle : 2 * middle],
            [pltpu.roll(x, depth // 2, 1) for x in corner] + packed[2 * middle :],
        ]
        for at, other in zip((y, y + half), theirs):
            mine = split(skewed_ref[at])
            right_ref[at] = join(
                [
                    jnp.where(lane + sub + k * SUB < cols, a, b)
                    for k, (a, b) in enumerate(zip(mine, other))
                ]
            )
        return carry

    lax.fori_loop(0, half, body, 0, unroll=2)


class Plan:
    def __init__(self, rows, cols):
        self.rows, self.cols = rows, cols
        self.half = cols // 2
        self.busy, self.slots = [], []
        for c in range(cols):
            busy = {self.step(c), self.step(cols - 1 - c)}
            busy |= {self.step(h) for h in (c - 1, cols - 2 - c) if h >= 0}
            if c in (self.half - 1, self.half):
                busy.add(self.half)
            free = [s for s in range(cols + 4 + rows) if s not in busy]
            self.busy.append(busy)
            self.slots.append(free[: rows - 1])
        last = [slots[-1] + 1 for slots in self.slots if slots]
        self.stages = max([cols] + last)

    def step(self, hop):
        return hop if hop < self.half else hop + 1

    def hop_at(self, s):
        if s == self.half:
            return None
        return s if s < self.half else s - 1

    def paths(self, hop):
        name = "first" if hop < self.half else "second"
        return [name, f"{name}_jumps"]

    def route(self, s):
        pairs = []
        for h in range(self.cols - 1):
            for r in range(self.rows):
                if self.step(h) == s:
                    pairs.append(((r, h), (r, h + 1)))
                    if h != self.half - 1:
                        pairs.append(((r, self.cols - 1 - h), (r, self.cols - 2 - h)))
        for c, slots in enumerate(self.slots):
            if s in slots:
                j = slots.index(s)
                pairs += [
                    ((j, c), (j + 1, c)),
                    ((self.rows - 1 - j, c), (self.rows - 2 - j, c)),
                ]
        return self.numbers(pairs)

    def crossed_route(self):
        return self.numbers([((r, self.half), (r, self.half - 1)) for r in range(self.rows)])

    def numbers(self, pairs):
        number = lambda place: place[0] * self.cols + place[1]
        return [(number(a), number(b)) for a, b in pairs]

    def turning(self, s):
        ends = {0, self.cols - 1}
        return [c for c in range(self.cols) if s == (1 if c in ends else 0)]

    def settling(self, s):
        found = []
        for c, slots in enumerate(self.slots):
            at = slots[-1] + 1
            while at < self.stages and at in self.busy[c]:
                at += 1
            if at == s:
                found.append(c)
        return found


def in_vmem(count):
    return [pl.BlockSpec(memory_space=pltpu.VMEM)] * count


def shards(costs, p_small, p_large):
    rows, cols, depth = costs.shape
    plan = Plan(lax.axis_size("row"), lax.axis_size("col"))
    params = {"vmem_limit_bytes": LIMIT}
    front = jax.ShapeDtypeStruct((depth, cols), jnp.bfloat16)
    tile = jax.ShapeDtypeStruct((rows, cols, depth), jnp.bfloat16)
    shapes = {
        "first": jax.ShapeDtypeStruct((rows, depth, cols), jnp.float32),
        "first_jumps": jax.ShapeDtypeStruct((rows, SUB, cols), jnp.float32),
        "second": jax.ShapeDtypeStruct((rows, depth, cols), jnp.float32),
        "second_jumps": jax.ShapeDtypeStruct((rows, SUB, cols), jnp.float32),
        "turned": jax.ShapeDtypeStruct((rows, depth, cols), jnp.bfloat16),
        "base": jax.ShapeDtypeStruct((rows, cols, depth), jnp.float32),
    }
    held = pltpu.VMEM((2, depth, cols), jnp.bfloat16)
    vsums = pltpu.VMEM((rows, depth, cols), jnp.bfloat16)

    tiles, lows, prices, near = pl.pallas_call(
        prepare_kernel,
        out_shape=(
            jax.ShapeDtypeStruct((cols, depth, cols), jnp.float32),
            jax.ShapeDtypeStruct((cols, SUB, cols), jnp.float32),
            jax.ShapeDtypeStruct((2, SUB, cols), jnp.float32),
            tile,
        ),
        in_specs=in_vmem(1) + [pl.BlockSpec(memory_space=pltpu.HBM)] * 2,
        out_specs=tuple(in_vmem(4)),
        scratch_shapes=[
            pltpu.VMEM((cols // SUB, depth, rows * SUB), jnp.bfloat16),
            pltpu.SMEM((2, 1), jnp.int32),
            pltpu.SemaphoreType.DMA((2,)),
        ],
        compiler_params=pltpu.CompilerParams(**params),
        name="prepare",
    )(costs, p_small, p_large)
    buffers = {"tiles": tiles, "lows": lows}

    def run(body, name, results, reads, writes, scratch):
        known = [n for n in writes if n in buffers]
        inputs = reads + known
        outputs = list(results) + writes
        names = [n for n in reads] + [f"{n}_before" for n in known] + outputs + list(scratch)
        lead = 2
        values = pl.pallas_call(
            functools.partial(body, names),
            out_shape=tuple([results[n] for n in results] + [shapes[n] for n in writes]),
            in_specs=in_vmem(lead + len(inputs)),
            out_specs=tuple(in_vmem(len(outputs))),
            scratch_shapes=list(scratch.values()),
            input_output_aliases={
                lead + len(reads) + n: outputs.index(name) for n, name in enumerate(known)
            },
            compiler_params=pltpu.CompilerParams(**params),
            name=name,
        )(prices, near, *[buffers[n] for n in inputs])
        buffers.update(zip(outputs, values))

    for s in range(plan.stages):
        hop = plan.hop_at(s)
        writes = plan.paths(hop) if hop is not None and hop < plan.cols - 1 else []
        writes += ["turned"] if s < 2 else []
        writes += ["base"] if plan.settling(s) else []
        reads = ["tiles", "lows"] + ([] if "turned" in writes else ["turned"])
        reads += [f"arrival{n}" for n in range(s)]
        reads += ["crossed"] if hop == plan.half else []
        run(
            functools.partial(stage_kernel, plan, s),
            f"stage{s}",
            {"sent": front},
            reads,
            writes,
            {"held": held, "vsums": vsums},
        )
        buffers[f"arrival{s}"] = lax.ppermute(buffers["sent"], ("row", "col"), plan.route(s))
        if s == plan.half - 1:
            route = plan.crossed_route()
            buffers["crossed"] = lax.ppermute(buffers["sent"], ("row", "col"), route)

    run(
        functools.partial(final_kernel, plan),
        "final",
        {
            "left": tile,
            "skewed": tile,
            "packed": jax.ShapeDtypeStruct((rows // 2, cols // 2 * 3, depth), jnp.bfloat16),
        },
        ["tiles", "lows", "turned", "first", "first_jumps"]
        + [f"arrival{n}" for n in range(plan.stages)],
        ["second", "second_jumps", "base"],
        {
            "held": held,
            "vsums": vsums,
            "natural": pltpu.VMEM((rows, cols, depth), jnp.float32),
        },
    )
    arrived = lax.ppermute(buffers["packed"], "col", [(i, i - 1) for i in range(1, plan.cols)])
    right_view = pl.pallas_call(
        merge_kernel,
        out_shape=tile,
        in_specs=in_vmem(2),
        out_specs=pl.BlockSpec(memory_space=pltpu.VMEM),
        compiler_params=pltpu.CompilerParams(**params),
        name="merge",
    )(buffers["skewed"], arrived)
    return buffers["left"], right_view


def solution(mesh):
    placed = (P("row", "col", None), P(), P())
    return jax.shard_map(
        shards,
        mesh=mesh,
        in_specs=placed,
        out_specs=(P("row", "col", None), P("row", "col", None)),
        check_vma=False,
    )
```

```python
import functools

import jax
import jax.numpy as jnp
from jax import lax
from jax.experimental import pallas as pl
from jax.experimental.pallas import tpu as pltpu
from jax.sharding import PartitionSpec as P

SUB = 8
BIG = 1e30
TRANSPOSED = (((1,), (1,)), ((), ()))
PLAIN = (((1,), (0,)), ((), ()))
LIMIT = 20 * 1024 * 1024


def one_hot(rule, size):
    row = lax.broadcasted_iota(jnp.int32, (size, size), 0)
    col = lax.broadcasted_iota(jnp.int32, (size, size), 1)
    return jnp.where(rule(row, col), 1.0, 0.0).astype(jnp.bfloat16)


def interleave(size):
    return one_hot(lambda r, c: c == (r % SUB) * (size // SUB) + r // SUB, size)


def identity(size):
    return one_hot(lambda r, c: r == c, size)


def dot(a, b, dims):
    return lax.dot_general(a, b, dims, preferred_element_type=jnp.float32)


def split(block):
    wide = block.astype(jnp.float32)
    return [wide[i : i + SUB] for i in range(0, wide.shape[0], SUB)]


def join(parts):
    return jnp.concatenate(parts, axis=0).astype(jnp.bfloat16)


def fold_min(parts):
    parts = list(parts)
    while len(parts) > 1:
        parts = [jnp.minimum(a, b) for a, b in zip(parts[::2], parts[1::2])]
    low = parts[0]
    for shift in (4, 2, 1):
        low = jnp.minimum(low, pltpu.roll(low, shift, 0))
    return low


def relax(v, q1, q2):
    sub = lax.broadcasted_iota(jnp.int32, v[0].shape, 0)
    under = jnp.where(sub == 0, BIG, pltpu.roll(v[-1], 1, 0))
    over = jnp.where(sub == SUB - 1, BIG, pltpu.roll(v[0], SUB - 1, 0))
    low = fold_min(v)
    jump = low + q2
    below = [under] + v[:-1]
    above = v[1:] + [over]
    best = [
        jnp.minimum(jnp.minimum(x, jump), jnp.minimum(a, b) + q1)
        for x, a, b in zip(v, below, above)
    ]
    return best, low


def penalties(prices_ref):
    return prices_ref[0], prices_ref[1]


def spread(rows, lanes, first):
    row = lax.broadcasted_iota(jnp.int32, (rows * SUB, 2 * lanes), 0)
    col = lax.broadcasted_iota(jnp.int32, (rows * SUB, 2 * lanes), 1)
    hit = row == (col % lanes % rows) * SUB + first + col // lanes
    return jnp.where(hit, 1.0, 0.0).astype(jnp.bfloat16)


def prepare_kernel(
    costs_ref, small_ref, large_ref,
    out_ref, low_ref, prices_ref, near_ref,
    mixed_ref, price_refs, arrived,
):
    rows, cols, depth = costs_ref.shape
    mix = interleave(depth)
    fetches = [
        pltpu.make_async_copy(ref, price_refs.at[n], arrived.at[n])
        for n, ref in enumerate((small_ref, large_ref))
    ]
    for fetch in fetches:
        fetch.start()

    def mixed(i, carry):
        at = pl.ds(pl.multiple_of(i * 2 * SUB, 2 * SUB), 2 * SUB)
        block = costs_ref[:, at, :]
        near_ref[:, at, :] = block
        wide = block.astype(jnp.float32)
        for n in range(2):
            part = wide[:, n * SUB : (n + 1) * SUB].reshape(rows * SUB, depth)
            flat = dot(mix, part.astype(jnp.bfloat16), TRANSPOSED)
            mixed_ref[2 * i + n] = flat.astype(jnp.bfloat16)
        return carry

    lax.fori_loop(0, cols // SUB // 2, mixed, 0, unroll=2)
    for j in range(0, SUB, 2):
        pick = spread(rows, cols, j)

        def body(i, carry):
            flat = dot(mixed_ref[i], pick, PLAIN)
            for n in range(2):
                part = flat[:, n * cols : (n + 1) * cols]
                out_ref[i * SUB + j + n] = part
                low_ref[i * SUB + j + n] = fold_min(split(part))
            return carry

        lax.fori_loop(0, cols // SUB, body, 0, unroll=4)

    for n, fetch in enumerate(fetches):
        fetch.wait()
        price = jnp.full(prices_ref.shape[1:], price_refs[n, 0], jnp.int32)
        prices_ref[n] = price.astype(jnp.float32)


def turn_rows(costs_ref, tiles_ref):
    rows, cols, depth = costs_ref.shape
    mix = interleave(depth)
    batch = 4

    def body(i, carry):
        block = costs_ref[pl.ds(i * batch, batch)].reshape(batch * cols, depth)
        flat = dot(mix, block, TRANSPOSED).astype(jnp.bfloat16)
        for n in range(batch):
            tiles_ref[i * batch + n] = flat[:, n * cols : (n + 1) * cols]
        return carry

    lax.fori_loop(0, rows // batch, body, 0, unroll=2)


def sweep(v, tiles_ref, lows_ref, raw_ref, jumps_ref, rows, west, q1, q2):
    cols, depth, lanes = tiles_ref.shape
    pack = lanes // rows
    lane = lax.broadcasted_iota(jnp.int32, (SUB, lanes), 1)
    sub = lax.broadcasted_iota(jnp.int32, (SUB, lanes), 0)
    groups = [jnp.where(west, pack - 1 - j, j) for j in range(pack)]
    mine = [(lane >= g * rows) & (lane < (g + 1) * rows) for g in groups]

    def body(i, carry):
        v, jump = list(carry[:-1]), carry[-1]
        at = jnp.where(west, cols // pack - 1 - i, i)
        for j in range(pack):
            x = at * pack + groups[j]
            c = split(tiles_ref[x])
            below = [jnp.where(sub == 0, BIG, pltpu.roll(v[-1], 1, 0))] + v[:-1]
            above = v[1:] + [jnp.where(sub == SUB - 1, BIG, pltpu.roll(v[0], SUB - 1, 0))]
            near = [
                jnp.minimum(n, jnp.minimum(a, b) + q1) for n, a, b in zip(v, below, above)
            ]
            best = [jnp.minimum(n, jump) for n in near]
            for k, x_best in enumerate(best):
                pltpu.store(raw_ref.at[at, pl.ds(k * SUB, SUB), :], x_best, mask=mine[j])
            pltpu.store(jumps_ref.at[at], jump, mask=mine[j])
            low = fold_min([n + k for n, k in zip(near, c)])
            v = [n + k for n, k in zip(best, c)]
            jump = jnp.minimum(low, lows_ref[x] + jump) + q2
        return tuple(v) + (jump,)

    last = lax.fori_loop(0, cols // pack, body, tuple(v) + (fold_min(v) + q2,))
    low = last[-1] - q2
    return [x - low for x in last[:-1]]


def descend(v, tiles_ref, north, q1, q2):
    rows = tiles_ref.shape[0]

    def body(i, v):
        best, _ = relax(list(v), q1, q2)
        at = jnp.where(north, rows - 1 - i, i)
        return tuple(a + b for a, b in zip(best, split(tiles_ref[at])))

    return list(lax.fori_loop(0, rows, body, tuple(v), unroll=4))


def settle(south, north, costs_ref, tiles_ref, sums_ref, base_ref, q1, q2):
    rows, cols, depth = costs_ref.shape
    count = len(south)

    def both(first, i, v):
        out = []
        for at, part in ((i, v[:count]), (rows - 1 - i, v[count:])):
            best, low = relax(list(part), q1, q2)
            extra = [x - low for x in best]
            if not first:
                extra = [a + b for a, b in zip(extra, split(sums_ref[at]))]
            sums_ref[at] = join(extra)
            out += [a + b for a, b in zip(best, split(tiles_ref[at]))]
        return tuple(out)

    v = lax.fori_loop(0, rows // 2, functools.partial(both, True), tuple(south + north), unroll=2)
    lax.fori_loop(rows // 2, rows, functools.partial(both, False), v, unroll=2)

    ident, mix = identity(cols), interleave(depth)
    batch = 4

    def body(i, carry):
        block = sums_ref[pl.ds(i * batch, batch)].reshape(batch * depth, cols)
        flat = dot(ident, block, TRANSPOSED).astype(jnp.bfloat16)
        for n in range(batch):
            y = i * batch + n
            extra = dot(flat[:, n * depth : (n + 1) * depth], mix, PLAIN)
            base_ref[y] = extra + 4.0 * costs_ref[y].astype(jnp.float32) + 2.0 * q2[:1]
        return carry

    lax.fori_loop(0, rows // batch, body, 0, unroll=2)


def lowered(v):
    low = fold_min(v)
    return [x - low for x in v]


def choose(table, here):
    found = jnp.int32(-1)
    for n, value in enumerate(table):
        found = jnp.where(here == n, jnp.int32(value), found)
    return found


def load_arrival(index, arrivals, held_ref):
    @pl.when(index < 0)
    def _():
        held_ref[...] = jnp.zeros(held_ref.shape, held_ref.dtype)

    for n, ref in enumerate(arrivals):

        @pl.when(index == n)
        def _():
            held_ref[...] = ref[...]


def load_verticals(plan, col_here, row_here, arrivals, held_ref):
    for n in range(2):
        hop = row_here - 1 if n == 0 else plan.rows - 2 - row_here
        source = jnp.int32(-1)
        for j in range(plan.rows - 1):
            found = choose([slots[j] for slots in plan.slots], col_here)
            source = jnp.where(hop == j, found, source)
        load_arrival(source, arrivals, held_ref.at[n])


def among(here, columns):
    hit = here == columns[0]
    for c in columns[1:]:
        hit = hit | (here == c)
    return hit


def stage_kernel(plan, s, names, prices_ref, costs_ref, *refs):
    refs = dict(zip(names, refs))
    arrivals = [refs[f"arrival{n}"] for n in range(s)]
    tiles_ref, turned_ref = refs["tiles"], refs["turned"]
    out_ref, held_ref = refs["sent"], refs["held"]
    rows, cols, depth = costs_ref.shape
    col_here, row_here = lax.axis_index("col"), lax.axis_index("row")
    q1, q2 = penalties(prices_ref)

    hop = plan.hop_at(s)
    if hop is not None and hop < plan.cols - 1:

        @pl.when((col_here == hop) | (col_here == plan.cols - 1 - hop))
        def _():
            west = col_here != hop
            if hop:
                v = split(arrivals[plan.step(hop - 1)][...])
                if hop == plan.half:
                    other = split(refs["crossed"][...])
                    v = [jnp.where(west, b, a) for a, b in zip(v, other)]
            else:
                v = [jnp.zeros((SUB, cols), jnp.float32)] * (depth // SUB)
            raw, jumps = (refs[n] for n in plan.paths(hop))
            out_ref[...] = join(sweep(v, tiles_ref, refs["lows"], raw, jumps, rows, west, q1, q2))

    turning = plan.turning(s)
    if turning:

        @pl.when(among(col_here, turning))
        def _():
            turn_rows(costs_ref, turned_ref)

    if any(s in slots for slots in plan.slots):
        hops = [slots.index(s) if s in slots else -1 for slots in plan.slots]
        source = [slots[j - 1] if j > 0 else -1 for slots, j in zip(plan.slots, hops)]
        hop = choose(hops, col_here)
        north = row_here == plan.rows - 1 - hop

        @pl.when((hop >= 0) & ((row_here == hop) | north))
        def _():
            load_arrival(choose(source, col_here), arrivals, held_ref.at[0])
            v = descend(split(held_ref[0]), turned_ref, north, q1, q2)
            out_ref[...] = join(lowered(v))

    settling = plan.settling(s)
    if settling:

        @pl.when(among(col_here, settling))
        def _():
            load_verticals(plan, col_here, row_here, arrivals, held_ref)
            south, north = split(held_ref[0]), split(held_ref[1])
            settle(south, north, costs_ref, turned_ref, refs["vsums"], refs["base"], q1, q2)


def skew(v, lane, sub):
    count = len(v)
    bit = 1
    while bit < SUB:
        taken = (lane & bit) != 0
        inner = sub < SUB - bit
        up = [pltpu.roll(a, SUB - bit, 0) for a in v]
        v = [
            jnp.where(taken, jnp.where(inner, up[k], up[(k + 1) % count]), v[k])
            for k in range(count)
        ]
        bit *= 2
    while bit < SUB * count:
        taken = (lane & bit) != 0
        v = [jnp.where(taken, v[(k + bit // SUB) % count], v[k]) for k in range(count)]
        bit *= 2
    return v


def final_kernel(plan, names, prices_ref, costs_ref, *refs):
    refs = dict(zip(names, refs))
    arrivals = [refs[f"arrival{n}"] for n in range(plan.stages)]
    rows, cols, depth = costs_ref.shape
    lanes = cols
    held_ref, base_ref, natural_ref = refs["held"], refs["base"], refs["natural"]
    q1, q2 = penalties(prices_ref)
    col_here, row_here = lax.axis_index("col"), lax.axis_index("row")

    late = plan.settling(plan.stages)
    if late:

        @pl.when(among(col_here, late))
        def _():
            load_verticals(plan, col_here, row_here, arrivals, held_ref)
            south, north = split(held_ref[0]), split(held_ref[1])
            settle(south, north, costs_ref, refs["turned"], refs["vsums"], base_ref, q1, q2)

    @pl.when((col_here == 0) | (col_here == plan.cols - 1))
    def _():
        v = split(arrivals[plan.step(plan.cols - 2)][...])
        raw, jumps = refs["second"], refs["second_jumps"]
        sweep(v, refs["tiles"], refs["lows"], raw, jumps, rows, col_here == 0, q1, q2)

    order, mix = interleave(2 * cols), interleave(depth)

    def added(at):
        total = None
        for name in ("first", "second"):
            jump = refs[f"{name}_jumps"][at]
            part = [x - jump for x in split(refs[name][at])]
            total = part if total is None else [a + b for a, b in zip(total, part)]
        return join(total)

    def turn(i, carry):
        pair = jnp.concatenate([added(2 * i), added(2 * i + 1)], axis=1)
        flat = dot(order, pair, TRANSPOSED).astype(jnp.bfloat16)
        at = pl.ds(pl.multiple_of(i * SUB, SUB), SUB)
        natural_ref[:, at, :] = dot(flat, mix, PLAIN).reshape(rows, SUB, depth)
        return carry

    lax.fori_loop(0, cols // SUB, turn, 0, unroll=4)

    lane = lax.broadcasted_iota(jnp.int32, (SUB, lanes), 1)
    sub = lax.broadcasted_iota(jnp.int32, (SUB, lanes), 0)
    half = rows // 2
    middle = cols // SUB // 2

    def finish(y, carry):
        turned = []
        for at in (y, y + half):
            summed = natural_ref[at] + base_ref[at]
            view = (summed * (1.0 / 64.0)).astype(jnp.bfloat16)
            refs["left"][at] = view
            turned.append(skew(split(view), lane, sub))
            refs["skewed"][at] = join(turned[-1])
        corner = [
            jnp.where(lane >= lanes // 2, a, pltpu.roll(b, lanes // 2, 1))
            for a, b in zip(turned[0][:middle], turned[1][:middle])
        ]
        refs["packed"][y] = join(corner + turned[0][middle:] + turned[1][middle:])
        return carry

    lax.fori_loop(0, half, finish, 0, unroll=4)


def merge_kernel(skewed_ref, packed_ref, right_ref):
    rows, cols, depth = skewed_ref.shape
    lane = lax.broadcasted_iota(jnp.int32, (SUB, depth), 1)
    sub = lax.broadcasted_iota(jnp.int32, (SUB, depth), 0)
    half = rows // 2
    middle = cols // SUB // 2

    def body(y, carry):
        packed = split(packed_ref[y])
        corner = packed[:middle]
        theirs = [
            corner + packed[middle : 2 * middle],
            [pltpu.roll(x, depth // 2, 1) for x in corner] + packed[2 * middle :],
        ]
        for at, other in zip((y, y + half), theirs):
            mine = split(skewed_ref[at])
            right_ref[at] = join(
                [
                    jnp.where(lane + sub + k * SUB < cols, a, b)
                    for k, (a, b) in enumerate(zip(mine, other))
                ]
            )
        return carry

    lax.fori_loop(0, half, body, 0, unroll=4)


class Plan:
    def __init__(self, rows, cols):
        self.rows, self.cols = rows, cols
        self.half = cols // 2
        self.busy, self.slots = [], []
        for c in range(cols):
            busy = {self.step(c), self.step(cols - 1 - c)}
            busy |= {self.step(h) for h in (c - 1, cols - 2 - c) if h >= 0}
            if c in (self.half - 1, self.half):
                busy.add(self.half)
            free = [s for s in range(cols + 4 + rows) if s not in busy]
            self.busy.append(busy)
            self.slots.append(free[: rows - 1])
        last = [slots[-1] + 1 for slots in self.slots if slots]
        self.stages = max([cols] + last)

    def step(self, hop):
        return hop if hop < self.half else hop + 1

    def hop_at(self, s):
        if s == self.half:
            return None
        return s if s < self.half else s - 1

    def paths(self, hop):
        name = "first" if hop < self.half else "second"
        return [name, f"{name}_jumps"]

    def route(self, s):
        pairs = []
        for h in range(self.cols - 1):
            for r in range(self.rows):
                if self.step(h) == s:
                    pairs.append(((r, h), (r, h + 1)))
                    if h != self.half - 1:
                        pairs.append(((r, self.cols - 1 - h), (r, self.cols - 2 - h)))
        for c, slots in enumerate(self.slots):
            if s in slots:
                j = slots.index(s)
                pairs += [
                    ((j, c), (j + 1, c)),
                    ((self.rows - 1 - j, c), (self.rows - 2 - j, c)),
                ]
        return self.numbers(pairs)

    def crossed_route(self):
        return self.numbers([((r, self.half), (r, self.half - 1)) for r in range(self.rows)])

    def numbers(self, pairs):
        number = lambda place: place[0] * self.cols + place[1]
        return [(number(a), number(b)) for a, b in pairs]

    def turning(self, s):
        ends = {0, self.cols - 1}
        return [c for c in range(self.cols) if s == (1 if c in ends else 0)]

    def settling(self, s):
        found = []
        for c, slots in enumerate(self.slots):
            at = slots[-1] + 1
            while at < self.stages and at in self.busy[c]:
                at += 1
            if at == s:
                found.append(c)
        return found


def in_vmem(count):
    return [pl.BlockSpec(memory_space=pltpu.VMEM)] * count


def shards(costs, p_small, p_large):
    rows, cols, depth = costs.shape
    plan = Plan(lax.axis_size("row"), lax.axis_size("col"))
    params = {"vmem_limit_bytes": LIMIT}
    front = jax.ShapeDtypeStruct((depth, cols), jnp.bfloat16)
    tile = jax.ShapeDtypeStruct((rows, cols, depth), jnp.bfloat16)
    shapes = {
        "first": jax.ShapeDtypeStruct((rows, depth, cols), jnp.float32),
        "first_jumps": jax.ShapeDtypeStruct((rows, SUB, cols), jnp.float32),
        "second": jax.ShapeDtypeStruct((rows, depth, cols), jnp.float32),
        "second_jumps": jax.ShapeDtypeStruct((rows, SUB, cols), jnp.float32),
        "turned": jax.ShapeDtypeStruct((rows, depth, cols), jnp.bfloat16),
        "base": jax.ShapeDtypeStruct((rows, cols, depth), jnp.float32),
    }
    held = pltpu.VMEM((2, depth, cols), jnp.bfloat16)
    vsums = pltpu.VMEM((rows, depth, cols), jnp.bfloat16)

    tiles, lows, prices, near = pl.pallas_call(
        prepare_kernel,
        out_shape=(
            jax.ShapeDtypeStruct((cols, depth, cols), jnp.float32),
            jax.ShapeDtypeStruct((cols, SUB, cols), jnp.float32),
            jax.ShapeDtypeStruct((2, SUB, cols), jnp.float32),
            tile,
        ),
        in_specs=in_vmem(1) + [pl.BlockSpec(memory_space=pltpu.HBM)] * 2,
        out_specs=tuple(in_vmem(4)),
        scratch_shapes=[
            pltpu.VMEM((cols // SUB, depth, rows * SUB), jnp.bfloat16),
            pltpu.SMEM((2, 1), jnp.int32),
            pltpu.SemaphoreType.DMA((2,)),
        ],
        compiler_params=pltpu.CompilerParams(**params),
        name="prepare",
    )(costs, p_small, p_large)
    buffers = {"tiles": tiles, "lows": lows}

    def run(body, name, results, reads, writes, scratch):
        known = [n for n in writes if n in buffers]
        inputs = reads + known
        outputs = list(results) + writes
        names = [n for n in reads] + [f"{n}_before" for n in known] + outputs + list(scratch)
        lead = 2
        values = pl.pallas_call(
            functools.partial(body, names),
            out_shape=tuple([results[n] for n in results] + [shapes[n] for n in writes]),
            in_specs=in_vmem(lead + len(inputs)),
            out_specs=tuple(in_vmem(len(outputs))),
            scratch_shapes=list(scratch.values()),
            input_output_aliases={
                lead + len(reads) + n: outputs.index(name) for n, name in enumerate(known)
            },
            compiler_params=pltpu.CompilerParams(**params),
            name=name,
        )(prices, near, *[buffers[n] for n in inputs])
        buffers.update(zip(outputs, values))

    for s in range(plan.stages):
        hop = plan.hop_at(s)
        writes = plan.paths(hop) if hop is not None and hop < plan.cols - 1 else []
        writes += ["turned"] if s < 2 else []
        writes += ["base"] if plan.settling(s) else []
        reads = ["tiles", "lows"] + ([] if "turned" in writes else ["turned"])
        reads += [f"arrival{n}" for n in range(s)]
        reads += ["crossed"] if hop == plan.half else []
        run(
            functools.partial(stage_kernel, plan, s),
            f"stage{s}",
            {"sent": front},
            reads,
            writes,
            {"held": held, "vsums": vsums},
        )
        buffers[f"arrival{s}"] = lax.ppermute(buffers["sent"], ("row", "col"), plan.route(s))
        if s == plan.half - 1:
            route = plan.crossed_route()
            buffers["crossed"] = lax.ppermute(buffers["sent"], ("row", "col"), route)

    run(
        functools.partial(final_kernel, plan),
        "final",
        {
            "left": tile,
            "skewed": tile,
            "packed": jax.ShapeDtypeStruct((rows // 2, cols // 2 * 3, depth), jnp.bfloat16),
        },
        ["tiles", "lows", "turned", "first", "first_jumps"]
        + [f"arrival{n}" for n in range(plan.stages)],
        ["second", "second_jumps", "base"],
        {
            "held": held,
            "vsums": vsums,
            "natural": pltpu.VMEM((rows, cols, depth), jnp.float32),
        },
    )
    arrived = lax.ppermute(buffers["packed"], "col", [(i, i - 1) for i in range(1, plan.cols)])
    right_view = pl.pallas_call(
        merge_kernel,
        out_shape=tile,
        in_specs=in_vmem(2),
        out_specs=pl.BlockSpec(memory_space=pltpu.VMEM),
        compiler_params=pltpu.CompilerParams(**params),
        name="merge",
    )(buffers["skewed"], arrived)
    return buffers["left"], right_view


def solution(mesh):
    placed = (P("row", "col", None), P(), P())
    return jax.shard_map(
        shards,
        mesh=mesh,
        in_specs=placed,
        out_specs=(P("row", "col", None), P("row", "col", None)),
        check_vma=False,
    )
```

```python
import functools

import jax
import jax.numpy as jnp
from jax import lax
from jax.experimental import pallas as pl
from jax.experimental.pallas import tpu as pltpu
from jax.sharding import PartitionSpec as P

SUB = 8
BIG = 1e30
TRANSPOSED = (((1,), (1,)), ((), ()))
PLAIN = (((1,), (0,)), ((), ()))
LIMIT = 20 * 1024 * 1024


def one_hot(rule, size):
    row = lax.broadcasted_iota(jnp.int32, (size, size), 0)
    col = lax.broadcasted_iota(jnp.int32, (size, size), 1)
    return jnp.where(rule(row, col), 1.0, 0.0).astype(jnp.bfloat16)


def interleave(size):
    return one_hot(lambda r, c: c == (r % SUB) * (size // SUB) + r // SUB, size)


def identity(size):
    return one_hot(lambda r, c: r == c, size)


def dot(a, b, dims):
    return lax.dot_general(a, b, dims, preferred_element_type=jnp.float32)


def split(block):
    wide = block.astype(jnp.float32)
    return [wide[i : i + SUB] for i in range(0, wide.shape[0], SUB)]


def join(parts):
    return jnp.concatenate(parts, axis=0).astype(jnp.bfloat16)


def fold_min(parts):
    parts = list(parts)
    while len(parts) > 1:
        parts = [jnp.minimum(a, b) for a, b in zip(parts[::2], parts[1::2])]
    low = parts[0]
    for shift in (4, 2, 1):
        low = jnp.minimum(low, pltpu.roll(low, shift, 0))
    return low


def relax(v, q1, q2):
    sub = lax.broadcasted_iota(jnp.int32, v[0].shape, 0)
    under = jnp.where(sub == 0, BIG, pltpu.roll(v[-1], 1, 0))
    over = jnp.where(sub == SUB - 1, BIG, pltpu.roll(v[0], SUB - 1, 0))
    low = fold_min(v)
    jump = low + q2
    below = [under] + v[:-1]
    above = v[1:] + [over]
    best = [
        jnp.minimum(jnp.minimum(x, jump), jnp.minimum(a, b) + q1)
        for x, a, b in zip(v, below, above)
    ]
    return best, low


def penalties(prices_ref):
    return prices_ref[0], prices_ref[1]


def spread(rows, lanes, first):
    row = lax.broadcasted_iota(jnp.int32, (rows * SUB, 2 * lanes), 0)
    col = lax.broadcasted_iota(jnp.int32, (rows * SUB, 2 * lanes), 1)
    hit = row == (col % lanes % rows) * SUB + first + col // lanes
    return jnp.where(hit, 1.0, 0.0).astype(jnp.bfloat16)


def prepare_kernel(
    costs_ref, small_ref, large_ref,
    out_ref, low_ref, prices_ref, near_ref,
    mixed_ref, price_refs, arrived,
):
    rows, cols, depth = costs_ref.shape
    mix = interleave(depth)
    fetches = [
        pltpu.make_async_copy(ref, price_refs.at[n], arrived.at[n])
        for n, ref in enumerate((small_ref, large_ref))
    ]
    for fetch in fetches:
        fetch.start()

    def mixed(i, carry):
        at = pl.ds(pl.multiple_of(i * 2 * SUB, 2 * SUB), 2 * SUB)
        block = costs_ref[:, at, :]
        near_ref[:, at, :] = block
        wide = block.astype(jnp.float32)
        for n in range(2):
            part = wide[:, n * SUB : (n + 1) * SUB].reshape(rows * SUB, depth)
            flat = dot(mix, part.astype(jnp.bfloat16), TRANSPOSED)
            mixed_ref[2 * i + n] = flat.astype(jnp.bfloat16)
        return carry

    lax.fori_loop(0, cols // SUB // 2, mixed, 0, unroll=4)
    for j in range(0, SUB, 2):
        pick = spread(rows, cols, j)

        def body(i, carry):
            flat = dot(mixed_ref[i], pick, PLAIN)
            for n in range(2):
                part = flat[:, n * cols : (n + 1) * cols]
                out_ref[i * SUB + j + n] = part
                low_ref[i * SUB + j + n] = fold_min(split(part))
            return carry

        lax.fori_loop(0, cols // SUB, body, 0, unroll=8)

    for n, fetch in enumerate(fetches):
        fetch.wait()
        price = jnp.full(prices_ref.shape[1:], price_refs[n, 0], jnp.int32)
        prices_ref[n] = price.astype(jnp.float32)


def turn_rows(costs_ref, tiles_ref):
    rows, cols, depth = costs_ref.shape
    mix = interleave(depth)
    batch = 4

    def body(i, carry):
        block = costs_ref[pl.ds(i * batch, batch)].reshape(batch * cols, depth)
        flat = dot(mix, block, TRANSPOSED).astype(jnp.bfloat16)
        for n in range(batch):
            tiles_ref[i * batch + n] = flat[:, n * cols : (n + 1) * cols]
        return carry

    lax.fori_loop(0, rows // batch, body, 0, unroll=2)


def sweep(v, tiles_ref, lows_ref, raw_ref, jumps_ref, rows, west, q1, q2):
    cols, depth, lanes = tiles_ref.shape
    pack = lanes // rows
    lane = lax.broadcasted_iota(jnp.int32, (SUB, lanes), 1)
    sub = lax.broadcasted_iota(jnp.int32, (SUB, lanes), 0)
    groups = [jnp.where(west, pack - 1 - j, j) for j in range(pack)]
    mine = [(lane >= g * rows) & (lane < (g + 1) * rows) for g in groups]

    def body(i, carry):
        v, jump = list(carry[:-1]), carry[-1]
        at = jnp.where(west, cols // pack - 1 - i, i)
        for j in range(pack):
            x = at * pack + groups[j]
            c = split(tiles_ref[x])
            below = [jnp.where(sub == 0, BIG, pltpu.roll(v[-1], 1, 0))] + v[:-1]
            above = v[1:] + [jnp.where(sub == SUB - 1, BIG, pltpu.roll(v[0], SUB - 1, 0))]
            near = [
                jnp.minimum(n, jnp.minimum(a, b) + q1) for n, a, b in zip(v, below, above)
            ]
            best = [jnp.minimum(n, jump) for n in near]
            for k, x_best in enumerate(best):
                pltpu.store(raw_ref.at[at, pl.ds(k * SUB, SUB), :], x_best, mask=mine[j])
            pltpu.store(jumps_ref.at[at], jump, mask=mine[j])
            low = fold_min([n + k for n, k in zip(near, c)])
            v = [n + k for n, k in zip(best, c)]
            jump = jnp.minimum(low, lows_ref[x] + jump) + q2
        return tuple(v) + (jump,)

    last = lax.fori_loop(0, cols // pack, body, tuple(v) + (fold_min(v) + q2,))
    low = last[-1] - q2
    return [x - low for x in last[:-1]]


def descend(v, tiles_ref, north, q1, q2):
    rows = tiles_ref.shape[0]

    def body(i, v):
        best, _ = relax(list(v), q1, q2)
        at = jnp.where(north, rows - 1 - i, i)
        return tuple(a + b for a, b in zip(best, split(tiles_ref[at])))

    return list(lax.fori_loop(0, rows, body, tuple(v), unroll=4))


def settle(south, north, costs_ref, tiles_ref, sums_ref, base_ref, q1, q2):
    rows, cols, depth = costs_ref.shape
    count = len(south)

    def both(first, i, v):
        out = []
        for at, part in ((i, v[:count]), (rows - 1 - i, v[count:])):
            best, low = relax(list(part), q1, q2)
            extra = [x - low for x in best]
            if not first:
                extra = [a + b for a, b in zip(extra, split(sums_ref[at]))]
            sums_ref[at] = join(extra)
            out += [a + b for a, b in zip(best, split(tiles_ref[at]))]
        return tuple(out)

    v = lax.fori_loop(0, rows // 2, functools.partial(both, True), tuple(south + north), unroll=2)
    lax.fori_loop(rows // 2, rows, functools.partial(both, False), v, unroll=2)

    ident, mix = identity(cols), interleave(depth)
    batch = 4

    def body(i, carry):
        block = sums_ref[pl.ds(i * batch, batch)].reshape(batch * depth, cols)
        flat = dot(ident, block, TRANSPOSED).astype(jnp.bfloat16)
        for n in range(batch):
            y = i * batch + n
            extra = dot(flat[:, n * depth : (n + 1) * depth], mix, PLAIN)
            base_ref[y] = extra + 4.0 * costs_ref[y].astype(jnp.float32) + 2.0 * q2[:1]
        return carry

    lax.fori_loop(0, rows // batch, body, 0, unroll=2)


def lowered(v):
    low = fold_min(v)
    return [x - low for x in v]


def choose(table, here):
    found = jnp.int32(-1)
    for n, value in enumerate(table):
        found = jnp.where(here == n, jnp.int32(value), found)
    return found


def load_arrival(index, arrivals, held_ref):
    @pl.when(index < 0)
    def _():
        held_ref[...] = jnp.zeros(held_ref.shape, held_ref.dtype)

    for n, ref in enumerate(arrivals):

        @pl.when(index == n)
        def _():
            held_ref[...] = ref[...]


def load_verticals(plan, col_here, row_here, arrivals, held_ref):
    for n in range(2):
        hop = row_here - 1 if n == 0 else plan.rows - 2 - row_here
        source = jnp.int32(-1)
        for j in range(plan.rows - 1):
            found = choose([slots[j] for slots in plan.slots], col_here)
            source = jnp.where(hop == j, found, source)
        load_arrival(source, arrivals, held_ref.at[n])


def among(here, columns):
    hit = here == columns[0]
    for c in columns[1:]:
        hit = hit | (here == c)
    return hit


def stage_kernel(plan, s, names, prices_ref, costs_ref, *refs):
    refs = dict(zip(names, refs))
    arrivals = [refs[f"arrival{n}"] for n in range(s)]
    tiles_ref, turned_ref = refs["tiles"], refs["turned"]
    out_ref, held_ref = refs["sent"], refs["held"]
    rows, cols, depth = costs_ref.shape
    col_here, row_here = lax.axis_index("col"), lax.axis_index("row")
    q1, q2 = penalties(prices_ref)

    hop = plan.hop_at(s)
    if hop is not None and hop < plan.cols - 1:

        @pl.when((col_here == hop) | (col_here == plan.cols - 1 - hop))
        def _():
            west = col_here != hop
            if hop:
                v = split(arrivals[plan.step(hop - 1)][...])
                if hop == plan.half:
                    other = split(refs["crossed"][...])
                    v = [jnp.where(west, b, a) for a, b in zip(v, other)]
            else:
                v = [jnp.zeros((SUB, cols), jnp.float32)] * (depth // SUB)
            raw, jumps = (refs[n] for n in plan.paths(hop))
            out_ref[...] = join(sweep(v, tiles_ref, refs["lows"], raw, jumps, rows, west, q1, q2))

    turning = plan.turning(s)
    if turning:

        @pl.when(among(col_here, turning))
        def _():
            turn_rows(costs_ref, turned_ref)

    if any(s in slots for slots in plan.slots):
        hops = [slots.index(s) if s in slots else -1 for slots in plan.slots]
        source = [slots[j - 1] if j > 0 else -1 for slots, j in zip(plan.slots, hops)]
        hop = choose(hops, col_here)
        north = row_here == plan.rows - 1 - hop

        @pl.when((hop >= 0) & ((row_here == hop) | north))
        def _():
            load_arrival(choose(source, col_here), arrivals, held_ref.at[0])
            v = descend(split(held_ref[0]), turned_ref, north, q1, q2)
            out_ref[...] = join(lowered(v))

    settling = plan.settling(s)
    if settling:

        @pl.when(among(col_here, settling))
        def _():
            load_verticals(plan, col_here, row_here, arrivals, held_ref)
            south, north = split(held_ref[0]), split(held_ref[1])
            settle(south, north, costs_ref, turned_ref, refs["vsums"], refs["base"], q1, q2)


def skew(v, lane, sub):
    count = len(v)
    bit = 1
    while bit < SUB:
        taken = (lane & bit) != 0
        inner = sub < SUB - bit
        up = [pltpu.roll(a, SUB - bit, 0) for a in v]
        v = [
            jnp.where(taken, jnp.where(inner, up[k], up[(k + 1) % count]), v[k])
            for k in range(count)
        ]
        bit *= 2
    while bit < SUB * count:
        taken = (lane & bit) != 0
        v = [jnp.where(taken, v[(k + bit // SUB) % count], v[k]) for k in range(count)]
        bit *= 2
    return v


def final_kernel(plan, names, prices_ref, costs_ref, *refs):
    refs = dict(zip(names, refs))
    arrivals = [refs[f"arrival{n}"] for n in range(plan.stages)]
    rows, cols, depth = costs_ref.shape
    lanes = cols
    held_ref, base_ref, natural_ref = refs["held"], refs["base"], refs["natural"]
    q1, q2 = penalties(prices_ref)
    col_here, row_here = lax.axis_index("col"), lax.axis_index("row")

    late = plan.settling(plan.stages)
    if late:

        @pl.when(among(col_here, late))
        def _():
            load_verticals(plan, col_here, row_here, arrivals, held_ref)
            south, north = split(held_ref[0]), split(held_ref[1])
            settle(south, north, costs_ref, refs["turned"], refs["vsums"], base_ref, q1, q2)

    @pl.when((col_here == 0) | (col_here == plan.cols - 1))
    def _():
        v = split(arrivals[plan.step(plan.cols - 2)][...])
        raw, jumps = refs["second"], refs["second_jumps"]
        sweep(v, refs["tiles"], refs["lows"], raw, jumps, rows, col_here == 0, q1, q2)

    order, mix = interleave(2 * cols), interleave(depth)

    def added(at):
        total = None
        for name in ("first", "second"):
            jump = refs[f"{name}_jumps"][at]
            part = [x - jump for x in split(refs[name][at])]
            total = part if total is None else [a + b for a, b in zip(total, part)]
        return join(total)

    def turn(i, carry):
        pair = jnp.concatenate([added(2 * i), added(2 * i + 1)], axis=1)
        flat = dot(order, pair, TRANSPOSED).astype(jnp.bfloat16)
        at = pl.ds(pl.multiple_of(i * SUB, SUB), SUB)
        natural_ref[:, at, :] = dot(flat, mix, PLAIN).reshape(rows, SUB, depth)
        return carry

    lax.fori_loop(0, cols // SUB, turn, 0, unroll=4)

    lane = lax.broadcasted_iota(jnp.int32, (SUB, lanes), 1)
    sub = lax.broadcasted_iota(jnp.int32, (SUB, lanes), 0)
    half = rows // 2
    middle = cols // SUB // 2

    def finish(y, carry):
        turned = []
        for at in (y, y + half):
            summed = natural_ref[at] + base_ref[at]
            view = (summed * (1.0 / 64.0)).astype(jnp.bfloat16)
            refs["left"][at] = view
            turned.append(skew(split(view), lane, sub))
            refs["skewed"][at] = join(turned[-1])
        corner = [
            jnp.where(lane >= lanes // 2, a, pltpu.roll(b, lanes // 2, 1))
            for a, b in zip(turned[0][:middle], turned[1][:middle])
        ]
        refs["packed"][y] = join(corner + turned[0][middle:] + turned[1][middle:])
        return carry

    lax.fori_loop(0, half, finish, 0, unroll=4)


def merge_kernel(skewed_ref, packed_ref, right_ref):
    rows, cols, depth = skewed_ref.shape
    lane = lax.broadcasted_iota(jnp.int32, (SUB, depth), 1)
    sub = lax.broadcasted_iota(jnp.int32, (SUB, depth), 0)
    half = rows // 2
    middle = cols // SUB // 2

    def body(y, carry):
        packed = split(packed_ref[y])
        corner = packed[:middle]
        theirs = [
            corner + packed[middle : 2 * middle],
            [pltpu.roll(x, depth // 2, 1) for x in corner] + packed[2 * middle :],
        ]
        for at, other in zip((y, y + half), theirs):
            mine = split(skewed_ref[at])
            right_ref[at] = join(
                [
                    jnp.where(lane + sub + k * SUB < cols, a, b)
                    for k, (a, b) in enumerate(zip(mine, other))
                ]
            )
        return carry

    lax.fori_loop(0, half, body, 0, unroll=4)


class Plan:
    def __init__(self, rows, cols):
        self.rows, self.cols = rows, cols
        self.half = cols // 2
        self.busy, self.slots = [], []
        for c in range(cols):
            busy = {self.step(c), self.step(cols - 1 - c)}
            busy |= {self.step(h) for h in (c - 1, cols - 2 - c) if h >= 0}
            if c in (self.half - 1, self.half):
                busy.add(self.half)
            free = [s for s in range(cols + 4 + rows) if s not in busy]
            self.busy.append(busy)
            self.slots.append(free[: rows - 1])
        last = [slots[-1] + 1 for slots in self.slots if slots]
        self.stages = max([cols] + last)

    def step(self, hop):
        return hop if hop < self.half else hop + 1

    def hop_at(self, s):
        if s == self.half:
            return None
        return s if s < self.half else s - 1

    def paths(self, hop):
        name = "first" if hop < self.half else "second"
        return [name, f"{name}_jumps"]

    def route(self, s):
        pairs = []
        for h in range(self.cols - 1):
            for r in range(self.rows):
                if self.step(h) == s:
                    pairs.append(((r, h), (r, h + 1)))
                    if h != self.half - 1:
                        pairs.append(((r, self.cols - 1 - h), (r, self.cols - 2 - h)))
        for c, slots in enumerate(self.slots):
            if s in slots:
                j = slots.index(s)
                pairs += [
                    ((j, c), (j + 1, c)),
                    ((self.rows - 1 - j, c), (self.rows - 2 - j, c)),
                ]
        return self.numbers(pairs)

    def crossed_route(self):
        return self.numbers([((r, self.half), (r, self.half - 1)) for r in range(self.rows)])

    def numbers(self, pairs):
        number = lambda place: place[0] * self.cols + place[1]
        return [(number(a), number(b)) for a, b in pairs]

    def turning(self, s):
        ends = {0, self.cols - 1}
        return [c for c in range(self.cols) if s == (1 if c in ends else 0)]

    def settling(self, s):
        found = []
        for c, slots in enumerate(self.slots):
            at = slots[-1] + 1
            while at < self.stages and at in self.busy[c]:
                at += 1
            if at == s:
                found.append(c)
        return found


def in_vmem(count):
    return [pl.BlockSpec(memory_space=pltpu.VMEM)] * count


def shards(costs, p_small, p_large):
    rows, cols, depth = costs.shape
    plan = Plan(lax.axis_size("row"), lax.axis_size("col"))
    params = {"vmem_limit_bytes": LIMIT}
    front = jax.ShapeDtypeStruct((depth, cols), jnp.bfloat16)
    tile = jax.ShapeDtypeStruct((rows, cols, depth), jnp.bfloat16)
    shapes = {
        "first": jax.ShapeDtypeStruct((rows, depth, cols), jnp.float32),
        "first_jumps": jax.ShapeDtypeStruct((rows, SUB, cols), jnp.float32),
        "second": jax.ShapeDtypeStruct((rows, depth, cols), jnp.float32),
        "second_jumps": jax.ShapeDtypeStruct((rows, SUB, cols), jnp.float32),
        "turned": jax.ShapeDtypeStruct((rows, depth, cols), jnp.bfloat16),
        "base": jax.ShapeDtypeStruct((rows, cols, depth), jnp.float32),
    }
    held = pltpu.VMEM((2, depth, cols), jnp.bfloat16)
    vsums = pltpu.VMEM((rows, depth, cols), jnp.bfloat16)

    tiles, lows, prices, near = pl.pallas_call(
        prepare_kernel,
        out_shape=(
            jax.ShapeDtypeStruct((cols, depth, cols), jnp.float32),
            jax.ShapeDtypeStruct((cols, SUB, cols), jnp.float32),
            jax.ShapeDtypeStruct((2, SUB, cols), jnp.float32),
            tile,
        ),
        in_specs=in_vmem(1) + [pl.BlockSpec(memory_space=pltpu.HBM)] * 2,
        out_specs=tuple(in_vmem(4)),
        scratch_shapes=[
            pltpu.VMEM((cols // SUB, depth, rows * SUB), jnp.bfloat16),
            pltpu.SMEM((2, 1), jnp.int32),
            pltpu.SemaphoreType.DMA((2,)),
        ],
        compiler_params=pltpu.CompilerParams(**params),
        name="prepare",
    )(costs, p_small, p_large)
    buffers = {"tiles": tiles, "lows": lows}

    def run(body, name, results, reads, writes, scratch):
        known = [n for n in writes if n in buffers]
        inputs = reads + known
        outputs = list(results) + writes
        names = [n for n in reads] + [f"{n}_before" for n in known] + outputs + list(scratch)
        lead = 2
        values = pl.pallas_call(
            functools.partial(body, names),
            out_shape=tuple([results[n] for n in results] + [shapes[n] for n in writes]),
            in_specs=in_vmem(lead + len(inputs)),
            out_specs=tuple(in_vmem(len(outputs))),
            scratch_shapes=list(scratch.values()),
            input_output_aliases={
                lead + len(reads) + n: outputs.index(name) for n, name in enumerate(known)
            },
            compiler_params=pltpu.CompilerParams(**params),
            name=name,
        )(prices, near, *[buffers[n] for n in inputs])
        buffers.update(zip(outputs, values))

    for s in range(plan.stages):
        hop = plan.hop_at(s)
        writes = plan.paths(hop) if hop is not None and hop < plan.cols - 1 else []
        writes += ["turned"] if s < 2 else []
        writes += ["base"] if plan.settling(s) else []
        reads = ["tiles", "lows"] + ([] if "turned" in writes else ["turned"])
        reads += [f"arrival{n}" for n in range(s)]
        reads += ["crossed"] if hop == plan.half else []
        run(
            functools.partial(stage_kernel, plan, s),
            f"stage{s}",
            {"sent": front},
            reads,
            writes,
            {"held": held, "vsums": vsums},
        )
        buffers[f"arrival{s}"] = lax.ppermute(buffers["sent"], ("row", "col"), plan.route(s))
        if s == plan.half - 1:
            route = plan.crossed_route()
            buffers["crossed"] = lax.ppermute(buffers["sent"], ("row", "col"), route)

    run(
        functools.partial(final_kernel, plan),
        "final",
        {
            "left": tile,
            "skewed": tile,
            "packed": jax.ShapeDtypeStruct((rows // 2, cols // 2 * 3, depth), jnp.bfloat16),
        },
        ["tiles", "lows", "turned", "first", "first_jumps"]
        + [f"arrival{n}" for n in range(plan.stages)],
        ["second", "second_jumps", "base"],
        {
            "held": held,
            "vsums": vsums,
            "natural": pltpu.VMEM((rows, cols, depth), jnp.float32),
        },
    )
    arrived = lax.ppermute(buffers["packed"], "col", [(i, i - 1) for i in range(1, plan.cols)])
    right_view = pl.pallas_call(
        merge_kernel,
        out_shape=tile,
        in_specs=in_vmem(2),
        out_specs=pl.BlockSpec(memory_space=pltpu.VMEM),
        compiler_params=pltpu.CompilerParams(**params),
        name="merge",
    )(buffers["skewed"], arrived)
    return buffers["left"], right_view


def solution(mesh):
    placed = (P("row", "col", None), P(), P())
    return jax.shard_map(
        shards,
        mesh=mesh,
        in_specs=placed,
        out_specs=(P("row", "col", None), P("row", "col", None)),
        check_vma=False,
    )
```
